256 devices in a mesh: dp: 32 (over y, x, core), cluster: 8 (over z).
Axes of the slice: x: 4, y: 4, z: 8, core: 2. Of those that a mesh axis runs over, the one named last changes fastest.
Arguments:
- embeddings: bfloat16 [65536, 1024], P('dp'), as said below
- centroids: bfloat16 [8192, 1024], P('cluster'), as said below
Outputs:
- new_centroids: float32 [8192, 1024], P('cluster', 'dp')
Inputs may be any that keep to these rules, and one draw needn't show every extreme that they name: `embeddings`: every row is nonzero. `centroids`: every row is nonzero.
All inputs are finite; a program needn't handle non-finite values.
Results may differ from the reference program's by a relative error of at most 0.00045.
The reference program's roundings to bfloat16 on the way (of `unit_rows`, `unit_centroids` and `weights`) count: a program that leaves them out, or rounds other values in their place, can miss the bound.
Values sent between devices are 32-bit elements; how exact they have to be, the bound alone decides.
No kernel may reach another device: no remote copies, remote signals or barrier semaphores. Data moves between devices by JAX's collectives and lax.ppermute only.
A program may use at most 64 MiB of HBM per device.

```python
import jax
import jax.numpy as jnp
from jax import lax

D = 1024
K = 8192
SCALING_PASSES = 3
N = 65536


def shared_features(key):
    first, second = jax.random.split(key)
    unit_direction = jax.random.normal(first, (D,), jnp.float32)
    column_factor = jnp.exp(jax.random.uniform(second, (D,), jnp.float32, 0.0, 2.302585))
    return (unit_direction, column_factor)


def draw_embeddings(key, part):
    unit_direction, column_factor = shared_features(key)
    key = jax.random.fold_in(key, 11)
    first, second, third = jax.random.split(key, 3)
    position = jnp.arange(N, dtype=jnp.float32) / N
    affinity_strength = (0.3 + 0.9 * position) * jax.random.uniform(second, (N,), jnp.float32, 0.5, 1.5)
    noise = jnp.clip(jax.random.normal(first, (N, D), jnp.float32), -4.0, 4.0)
    row_multiplier = jnp.exp(jax.random.uniform(third, (N,), jnp.float32, 0.0, 2.302585))
    values = (noise + affinity_strength[:, None] * unit_direction[None, :]) * column_factor[None, :]
    return (values * row_multiplier[:, None]).astype(jnp.bfloat16)


def draw_centroids(key, part):
    unit_direction, column_factor = shared_features(key)
    key = jax.random.fold_in(key, 23)
    first, second, third = jax.random.split(key, 3)
    affinity_strength = jax.random.uniform(second, (K,), jnp.float32, 0.0, 1.5)
    noise = jnp.clip(jax.random.normal(first, (K, D), jnp.float32), -4.0, 4.0)
    row_multiplier = jnp.exp(jax.random.uniform(third, (K,), jnp.float32, 0.0, 2.302585))
    values = (noise + affinity_strength[:, None] * unit_direction[None, :]) * column_factor[None, :]
    return (values * row_multiplier[:, None]).astype(jnp.bfloat16)


def setup_inputs(seed: int = 0) -> dict:
    streams_of = jax.random.split(jax.random.key(seed), 3)
    return {
        "embeddings": draw_embeddings(jax.random.fold_in(streams_of[2], 71), 0),
        "centroids": draw_centroids(jax.random.fold_in(streams_of[2], 71), 0),
    }


SOFTNESS_LEVEL = 0.025

def normalize_rows(matrix):
    values = matrix.astype(jnp.float32)
    factor = lax.rsqrt(lax.optimization_barrier(jnp.mean(values * values, axis=1, keepdims=True)) + 1e-06)
    return (values * factor * matrix.shape[1] ** (-0.5)).astype(jnp.bfloat16)

def reference(embeddings, centroids):
    unit_rows = normalize_rows(embeddings)
    unit_centroids = normalize_rows(centroids)
    cosine_similarity = jnp.dot(unit_rows, unit_centroids.T, preferred_element_type=jnp.float32)
    affinity_kernel = jnp.exp((cosine_similarity - 1.0) / SOFTNESS_LEVEL)
    target = embeddings.shape[0] / centroids.shape[0]
    row_scale = jnp.ones((embeddings.shape[0],), jnp.float32)
    for repeat in range(SCALING_PASSES):
        column_scale = target / jnp.dot(row_scale, affinity_kernel, precision=lax.Precision.HIGHEST)
        row_scale = 1.0 / jnp.dot(affinity_kernel, column_scale, precision=lax.Precision.HIGHEST)
    weights = (row_scale[:, None] * affinity_kernel).astype(jnp.bfloat16)
    sums = jnp.dot(weights.T, unit_rows, preferred_element_type=jnp.float32)
    return sums * lax.rsqrt(lax.optimization_barrier(jnp.mean(sums * sums, axis=1, keepdims=True)) + 1e-06)
```

```python
import functools

import jax
import jax.numpy as jnp
from jax import lax
from jax.experimental import pallas as pl
from jax.experimental.pallas import tpu as pltpu
from jax.sharding import Mesh
from jax.sharding import PartitionSpec as P

SCALING_PASSES = 3
SOFTNESS_LEVEL = 0.025
LOG2_E = 1.4426950408889634
EXPONENT_SLOPE = LOG2_E / SOFTNESS_LEVEL
ROWS_DP = ("y", "x", "core")
LANES = 128
SUBLANES = 8

VMEM = pl.BlockSpec(memory_space=pltpu.VMEM)
SMEM = pl.BlockSpec(memory_space=pltpu.SMEM)


def resident(array):
    return pltpu.with_memory_space_constraint(array, pltpu.VMEM)


def params(**more):
    return pltpu.CompilerParams(vmem_limit_bytes=40 * 1024 * 1024, **more)


def unit(values):
    values = values.astype(jnp.float32)
    width = values.shape[1]
    factor = lax.rsqrt(jnp.mean(values * values, axis=1, keepdims=True) + 1e-06)
    return (values * factor * width ** (-0.5)).astype(jnp.bfloat16)


def share_order(chips_y, chips_x, share):
    order = []
    for x in range(chips_x):
        for y in range(chips_y):
            order.append((chips_x * y + x) * 2)
    for y in range(chips_y):
        for x in range(chips_x):
            order.append((chips_x * y + x) * 2 + 1)
    return order


def to_lanes(partial_ref, out_ref):
    copies = out_ref.shape[0]
    rows = []
    for group in range(partial_ref.shape[0] // LANES):
        block = partial_ref[group * LANES : (group + 1) * LANES, :]
        rows.append(jnp.sum(block.T, axis=0, keepdims=True))
    total = jnp.concatenate(rows, axis=0)
    for copy in range(copies):
        out_ref[copy] = total


def prepare_kernel(order, embeddings_ref, centroids_ref, kernel_ref, unit_ref, column_ref, centroid_scratch, partial):
    step = pl.program_id(0)
    chunk = embeddings_ref.shape[0]
    share = centroids_ref.shape[0] // len(order)

    @pl.when(step == 0)
    def _():
        for place, block in enumerate(order):
            centroid_scratch[place * share : (place + 1) * share, :] = unit(
                centroids_ref[block * share : (block + 1) * share, :]
            )
        partial[...] = jnp.zeros_like(partial)

    unit_rows = unit(embeddings_ref[...])
    start = pl.multiple_of(step * chunk, chunk)
    unit_ref[pl.ds(start, chunk), :] = unit_rows
    height = 256
    for part in range(centroid_scratch.shape[0] // height):
        rows = slice(part * height, (part + 1) * height)
        cosine = lax.dot_general(
            centroid_scratch[rows, :], unit_rows, (((1,), (1,)), ((), ())), preferred_element_type=jnp.float32
        )
        affinity = jnp.exp2((cosine - 1.0) * EXPONENT_SLOPE)
        kernel_ref[rows, pl.ds(start, chunk)] = affinity
        folded = affinity[:, :LANES]
        for tile in range(1, chunk // LANES):
            folded = folded + affinity[:, tile * LANES : (tile + 1) * LANES]
        partial[rows, :] += folded

    @pl.when(step == pl.num_programs(0) - 1)
    def _():
        to_lanes(partial, column_ref)


def row_kernel(target, columns_ref, kernel_ref, row_ref, scale_scratch):
    scale = target / jnp.sum(columns_ref[...], axis=0)
    for group in range(scale.shape[0]):
        scale_scratch[group * LANES : (group + 1) * LANES, :] = jnp.broadcast_to(
            scale[group : group + 1, :], (LANES, LANES)
        ).T
    centroids, rows = kernel_ref.shape
    tiles = rows // LANES
    height = 32

    def body(step, sums):
        start = pl.multiple_of(step * height, height)
        factor = scale_scratch[pl.ds(start, height), :]
        out = []
        for tile in range(tiles):
            product = kernel_ref[pl.ds(start, height), tile * LANES : (tile + 1) * LANES] * factor
            out.append(sums[tile] + jnp.sum(product.reshape(height // SUBLANES, SUBLANES, LANES), axis=0))
        return tuple(out)

    sums = lax.fori_loop(
        0, centroids // height, body, tuple(jnp.zeros((SUBLANES, LANES), jnp.float32) for _ in range(tiles))
    )
    total = jnp.concatenate([jnp.sum(tile, axis=0, keepdims=True) for tile in sums], axis=0)
    for copy in range(row_ref.shape[0]):
        row_ref[copy] = total


def column_kernel(rows_ref, kernel_ref, column_ref, partial):
    scale = 1.0 / jnp.sum(rows_ref[...], axis=0)
    centroids, rows = kernel_ref.shape
    tiles = rows // LANES
    height = 32
    factors = [jnp.broadcast_to(scale[tile : tile + 1, :], (SUBLANES, LANES)) for tile in range(tiles)]

    def body(step, carry):
        start = pl.multiple_of(step * height, height)
        total = None
        for tile in range(tiles):
            block = kernel_ref[pl.ds(start, height), tile * LANES : (tile + 1) * LANES]
            product = block.reshape(height // SUBLANES, SUBLANES, LANES) * factors[tile][None]
            total = product if total is None else total + product
        partial[pl.ds(start, height), :] = total.reshape(height, LANES)
        return carry

    lax.fori_loop(0, centroids // height, body, 0)
    to_lanes(partial, column_ref)


def weigh(kernel_ref, scale, weight_scratch, source, place, share):
    tiles = kernel_ref.shape[1] // LANES
    for tile in range(tiles):
        lanes = slice(tile * LANES, (tile + 1) * LANES)
        weight_scratch[place * share : (place + 1) * share, lanes] = (
            kernel_ref[pl.ds(source, share), lanes] * scale[tile : tile + 1, :]
        ).astype(jnp.bfloat16)


def sums_kernel(counts, place_ref, rows_ref, kernel_ref, unit_ref, *rest):
    outs, weight_scratch = rest[:-1], rest[-1]
    slow, fast = counts
    half = slow * fast
    share = kernel_ref.shape[0] // (2 * half)
    scale = 1.0 / jnp.sum(rows_ref[...], axis=0)
    base, first, second = place_ref[0], place_ref[1], place_ref[2]
    for a in range(slow):
        for b in range(fast):
            place = a * fast + b
            block = base * half + lax.rem(first + a, slow) * fast + lax.rem(second + b, fast)
            weigh(kernel_ref, scale, weight_scratch, pl.multiple_of(block * share, share), place, share)
    height = fast * share
    if len(outs) == 1:
        outs[0][...] = jnp.dot(weight_scratch[...], unit_ref[...], preferred_element_type=jnp.float32)
    else:
        for a in range(slow):
            outs[a][...] = jnp.dot(
                weight_scratch[a * height : (a + 1) * height, :], unit_ref[...], preferred_element_type=jnp.float32
            )


def add_kernel(parts, *refs):
    received_ref = refs[0]
    kept, outs = refs[1 : 1 + parts], refs[1 + parts :]
    height = kept[0].shape[0]
    for part in range(parts):
        outs[part][...] = kept[part][...] + received_ref[part * height : (part + 1) * height, :]


def fold_kernel(parts, *refs):
    ins, outs = refs[:-parts], refs[-parts:]
    share = outs[0].shape[0]
    for part in range(parts):
        rows = slice(part * share, (part + 1) * share)
        total = ins[0][rows, :]
        for other in ins[1:]:
            total = total + other[rows, :]
        outs[part][...] = total


def finish_kernel(*refs):
    ins, out_ref, turned = refs[:-2], refs[-2], refs[-1]
    total = ins[0][...]
    for other in ins[1:]:
        total = total + other[...]
    share, width = total.shape
    factor = lax.rsqrt(jnp.mean(total * total, axis=1, keepdims=True) + 1e-06)
    total = total * factor
    repeated = jnp.concatenate([total] * (LANES // share), axis=0)
    for group in range(width // LANES):
        turned[group * LANES : (group + 1) * LANES, :] = repeated[:, group * LANES : (group + 1) * LANES].T
    slab = lax.broadcasted_iota(jnp.int32, (SUBLANES, LANES), 1) // share
    features = width // out_ref.shape[0]
    slabs = features // SUBLANES
    for owner in range(out_ref.shape[0]):
        tile = turned[owner * features : owner * features + SUBLANES, :]
        for j in range(1, slabs):
            start = owner * features + j * SUBLANES
            tile = jnp.where(slab == j, turned[start : start + SUBLANES, :], tile)
        out_ref[owner] = tile


def place_kernel(tiles_ref, out_ref):
    owners = tiles_ref.shape[0]
    centroids, features = out_ref.shape
    share = centroids // owners
    per = LANES // share
    slab = lax.broadcasted_iota(jnp.int32, (SUBLANES, LANES), 1) // share
    for group in range(owners // per):
        slabs = []
        for j in range(features // SUBLANES):
            made = None
            for s in range(per):
                tile = tiles_ref[group * per + s]
                shift = (share * (s - j)) % LANES
                moved = pltpu.roll(tile, shift, 1) if shift else tile
                made = moved if made is None else jnp.where(slab == s, moved, made)
            slabs.append(made)
        block = jnp.concatenate(slabs + [jnp.zeros((LANES - features, LANES), jnp.float32)], axis=0)
        out_ref[group * LANES : (group + 1) * LANES, :] = block.T[:, :features]


def ring(count, step):
    return [(i, (i + step) % count) for i in range(count)]


def per_device(sizes, embeddings, centroids):
    chips_y, chips_x, cores, clusters = sizes
    owners = chips_y * chips_x * cores
    rows, width = embeddings.shape
    local = centroids.shape[0]
    share = local // owners
    target = rows * owners / (local * clusters)
    order = share_order(chips_y, chips_x, share)
    f32, bf16 = jnp.float32, jnp.bfloat16
    chunk = 256

    kernel, unit_rows, columns = pl.pallas_call(
        functools.partial(prepare_kernel, order),
        grid=(rows // chunk,),
        in_specs=[
            pl.BlockSpec((chunk, width), lambda i: (i, 0)),
            pl.BlockSpec((local, width), lambda i: (0, 0)),
        ],
        out_specs=[VMEM, VMEM, VMEM],
        out_shape=[
            pltpu.VMEM((local, rows), f32),
            pltpu.VMEM((rows, width), bf16),
            pltpu.VMEM((owners, local // LANES, LANES), f32),
        ],
        scratch_shapes=[pltpu.VMEM((local, width), bf16), pltpu.VMEM((local, LANES), f32)],
        compiler_params=params(),
        name="prepare",
    )(embeddings, centroids)

    def column_exchange(sums):
        return lax.all_to_all(sums, ROWS_DP, 0, 0)

    def row_exchange(sums):
        return lax.all_to_all(sums, "cluster", 0, 0)

    for sweep in range(SCALING_PASSES):
        if sweep:
            columns = pl.pallas_call(
                column_kernel,
                in_specs=[VMEM, VMEM],
                out_specs=VMEM,
                out_shape=pltpu.VMEM((owners, local // LANES, LANES), f32),
                scratch_shapes=[pltpu.VMEM((local, LANES), f32)],
                compiler_params=params(),
                name="columns",
            )(resident(row_sums), resident(kernel))
        columns = column_exchange(columns)
        row_sums = pl.pallas_call(
            functools.partial(row_kernel, target),
            in_specs=[VMEM, VMEM],
            out_specs=VMEM,
            out_shape=pltpu.VMEM((clusters, rows // LANES, LANES), f32),
            scratch_shapes=[pltpu.VMEM((local, LANES), f32)],
            compiler_params=params(),
            name="rows",
        )(resident(columns), resident(kernel))
        row_sums = row_exchange(row_sums)

    y, x, core = (lax.axis_index(name).astype(jnp.int32) for name in ROWS_DP)
    half = owners // cores * share

    def weighted(owner_core, parts):
        first = jnp.where(owner_core == 0, x, y)
        second = jnp.where(owner_core == 0, y, x)
        place = jnp.stack([owner_core, first, second])
        return pl.pallas_call(
            functools.partial(sums_kernel, (chips_x, chips_y)),
            in_specs=[SMEM, VMEM, VMEM, VMEM],
            out_specs=[VMEM] * parts,
            out_shape=[pltpu.VMEM((half // parts, width), f32)] * parts,
            scratch_shapes=[pltpu.VMEM((half, rows), bf16)],
            compiler_params=params(),
            cost_estimate=pl.CostEstimate(
                flops=2 * half * rows * width, bytes_accessed=4 * half * (rows + width), transcendentals=0
            ),
            name="sums",
        )(place, resident(row_sums), resident(kernel), resident(unit_rows))

    (given,) = weighted(1 - core, 1)
    received = lax.ppermute(given, "core", ring(2, 1))
    kept = weighted(core, chips_x)

    first_parts = pl.pallas_call(
        functools.partial(add_kernel, chips_x),
        in_specs=[VMEM] * (1 + chips_x),
        out_specs=[VMEM] * chips_x,
        out_shape=[pltpu.VMEM((half // chips_x, width), f32)] * chips_x,
        compiler_params=params(),
        name="cores",
    )(resident(received), *[resident(part) for part in kept])

    def stage(parts, x_core):
        got = [parts[0]]
        for k in (1, 3, 2):
            pairs = []
            for j in range(chips_y):
                for i in range(chips_x):
                    for c in range(cores):
                        if c == x_core:
                            to = (j * chips_x + (i + k) % chips_x) * cores + c
                        else:
                            to = ((j + k) % chips_y * chips_x + i) * cores + c
                        pairs.append(((j * chips_x + i) * cores + c, to))
            got.append(lax.ppermute(parts[k], ROWS_DP, pairs))
        return got

    got = stage(first_parts, 0)
    second_parts = pl.pallas_call(
        functools.partial(fold_kernel, chips_y),
        in_specs=[VMEM] * len(got),
        out_specs=[VMEM] * chips_y,
        out_shape=[pltpu.VMEM((share, width), f32)] * chips_y,
        compiler_params=params(),
        name="fold",
    )(*[resident(part) for part in got])
    got = stage(second_parts, 1)
    tiles = pl.pallas_call(
        finish_kernel,
        in_specs=[VMEM] * len(got),
        out_specs=VMEM,
        out_shape=pltpu.VMEM((owners, SUBLANES, LANES), f32),
        scratch_shapes=[pltpu.VMEM((width, LANES), f32)],
        compiler_params=params(),
        name="finish",
    )(*[resident(part) for part in got])
    tiles = lax.all_to_all(tiles, ROWS_DP, 0, 0)
    return pl.pallas_call(
        place_kernel,
        in_specs=[VMEM],
        out_specs=VMEM,
        out_shape=jax.ShapeDtypeStruct((local, width // owners), f32),
        compiler_params=params(),
        name="place",
    )(resident(tiles))


def solution(mesh):
    clusters = mesh.shape["cluster"]
    sizes = (4, 4, 2, clusters)
    split = Mesh(mesh.devices.reshape(sizes), ROWS_DP + ("cluster",))
    return jax.shard_map(
        functools.partial(per_device, sizes),
        mesh=split,
        in_specs=(P(ROWS_DP, None), P("cluster", None)),
        out_specs=P("cluster", ROWS_DP),
        check_vma=False,
    )
```

```python
import functools

import jax
import jax.numpy as jnp
from jax import lax
from jax.experimental import pallas as pl
from jax.experimental.pallas import tpu as pltpu
from jax.sharding import Mesh
from jax.sharding import PartitionSpec as P

SCALING_PASSES = 3
SOFTNESS_LEVEL = 0.025
LOG2_E = 1.4426950408889634
EXPONENT_SLOPE = LOG2_E / SOFTNESS_LEVEL
ROWS_DP = ("y", "x", "core")
LANES = 128
SUBLANES = 8

VMEM = pl.BlockSpec(memory_space=pltpu.VMEM)


def resident(array):
    return pltpu.with_memory_space_constraint(array, pltpu.VMEM)


def streamed(array):
    return pltpu.with_memory_space_constraint(array, pltpu.HBM)


def params(mebibytes=4):
    return pltpu.CompilerParams(vmem_limit_bytes=mebibytes * 1024 * 1024)


def unit(values):
    values = values.astype(jnp.float32)
    width = values.shape[1]
    factor = lax.rsqrt(jnp.mean(values * values, axis=1, keepdims=True) + 1e-06)
    return (values * factor * width ** (-0.5)).astype(jnp.bfloat16)


def share_order(chips_y, chips_x, share):
    order = []
    for x in range(chips_x):
        for y in range(chips_y):
            order.append((chips_x * y + x) * 2)
    for y in range(chips_y):
        for x in range(chips_x):
            order.append((chips_x * y + x) * 2 + 1)
    return order


def to_lanes(partial_ref, out_ref):
    copies = out_ref.shape[0]
    rows = []
    for group in range(partial_ref.shape[0] // LANES):
        block = partial_ref[group * LANES : (group + 1) * LANES, :]
        rows.append(jnp.sum(block.T, axis=0, keepdims=True))
    total = jnp.concatenate(rows, axis=0)
    for copy in range(copies):
        out_ref[copy] = total


def prepare_kernel(order, embeddings_ref, centroids_ref, kernel_ref, unit_ref, column_ref, centroid_scratch, partial):
    step = pl.program_id(0)
    chunk = embeddings_ref.shape[0]
    share = centroids_ref.shape[0] // len(order)

    @pl.when(step == 0)
    def _():
        for place, block in enumerate(order):
            centroid_scratch[place * share : (place + 1) * share, :] = unit(
                centroids_ref[block * share : (block + 1) * share, :]
            )
        partial[...] = jnp.zeros_like(partial)

    unit_rows = unit(embeddings_ref[...])
    start = pl.multiple_of(step * chunk, chunk)
    unit_ref[pl.ds(start, chunk), :] = unit_rows
    height = 256
    for part in range(centroid_scratch.shape[0] // height):
        rows = slice(part * height, (part + 1) * height)
        cosine = lax.dot_general(
            centroid_scratch[rows, :], unit_rows, (((1,), (1,)), ((), ())), preferred_element_type=jnp.float32
        )
        affinity = jnp.exp2((cosine - 1.0) * EXPONENT_SLOPE)
        kernel_ref[rows, pl.ds(start, chunk)] = affinity
        folded = affinity[:, :LANES]
        for tile in range(1, chunk // LANES):
            folded = folded + affinity[:, tile * LANES : (tile + 1) * LANES]
        partial[rows, :] += folded

    @pl.when(step == pl.num_programs(0) - 1)
    def _():
        to_lanes(partial, column_ref)


def row_kernel(target, columns_ref, kernel_ref, row_ref, scale_scratch):
    scale = target / jnp.sum(columns_ref[...], axis=0)
    for group in range(scale.shape[0]):
        scale_scratch[group * LANES : (group + 1) * LANES, :] = jnp.broadcast_to(
            scale[group : group + 1, :], (LANES, LANES)
        ).T
    centroids, rows = kernel_ref.shape
    tiles = rows // LANES
    height = 32

    def body(step, sums):
        start = pl.multiple_of(step * height, height)
        factor = scale_scratch[pl.ds(start, height), :]
        out = []
        for tile in range(tiles):
            product = kernel_ref[pl.ds(start, height), tile * LANES : (tile + 1) * LANES] * factor
            out.append(sums[tile] + jnp.sum(product.reshape(height // SUBLANES, SUBLANES, LANES), axis=0))
        return tuple(out)

    sums = lax.fori_loop(
        0, centroids // height, body, tuple(jnp.zeros((SUBLANES, LANES), jnp.float32) for _ in range(tiles))
    )
    total = jnp.concatenate([jnp.sum(tile, axis=0, keepdims=True) for tile in sums], axis=0)
    for copy in range(row_ref.shape[0]):
        row_ref[copy] = total


def column_kernel(rows_ref, kernel_ref, column_ref, partial):
    scale = 1.0 / jnp.sum(rows_ref[...], axis=0)
    centroids, rows = kernel_ref.shape
    tiles = rows // LANES
    height = 32
    factors = [jnp.broadcast_to(scale[tile : tile + 1, :], (SUBLANES, LANES)) for tile in range(tiles)]

    def body(step, carry):
        start = pl.multiple_of(step * height, height)
        total = None
        for tile in range(tiles):
            block = kernel_ref[pl.ds(start, height), tile * LANES : (tile + 1) * LANES]
            product = block.reshape(height // SUBLANES, SUBLANES, LANES) * factors[tile][None]
            total = product if total is None else total + product
        partial[pl.ds(start, height), :] = total.reshape(height, LANES)
        return carry

    lax.fori_loop(0, centroids // height, body, 0)
    to_lanes(partial, column_ref)


def weigh(kernel_ref, scale, weight_scratch, source, place, share):
    tiles = kernel_ref.shape[1] // LANES
    for tile in range(tiles):
        lanes = slice(tile * LANES, (tile + 1) * LANES)
        weight_scratch[place * share : (place + 1) * share, lanes] = (
            kernel_ref[pl.ds(source, share), lanes] * scale[tile : tile + 1, :]
        ).astype(jnp.bfloat16)


def sums_kernel(counts, given, rows_ref, kernel_ref, unit_ref, *rest):
    outs, weight_scratch = rest[:-1], rest[-1]
    slow, fast = counts
    half = slow * fast
    share = kernel_ref.shape[0] // (2 * half)
    scale = 1.0 / jnp.sum(rows_ref[...], axis=0)
    y, x, core = (lax.axis_index(name) for name in ROWS_DP)
    base = 1 - core if given else core
    first, second = jnp.where(base == 0, x, y), jnp.where(base == 0, y, x)
    for a in range(slow):
        for b in range(fast):
            place = a * fast + b
            block = base * half + lax.rem(first + a, slow) * fast + lax.rem(second + b, fast)
            weigh(kernel_ref, scale, weight_scratch, pl.multiple_of(block * share, share), place, share)
    height = fast * share
    if len(outs) == 1:
        outs[0][...] = jnp.dot(weight_scratch[...], unit_ref[...], preferred_element_type=jnp.float32)
    else:
        for a in range(slow):
            outs[a][...] = jnp.dot(
                weight_scratch[a * height : (a + 1) * height, :], unit_ref[...], preferred_element_type=jnp.float32
            )


def add_kernel(parts, *refs):
    received_ref = refs[0]
    kept, outs = refs[1 : 1 + parts], refs[1 + parts :]
    height = kept[0].shape[0]
    for part in range(parts):
        outs[part][...] = kept[part][...] + received_ref[part * height : (part + 1) * height, :]


def fold_kernel(parts, *refs):
    ins, outs = refs[:-parts], refs[-parts:]
    share = outs[0].shape[0]
    for part in range(parts):
        rows = slice(part * share, (part + 1) * share)
        total = ins[0][rows, :]
        for other in ins[1:]:
            total = total + other[rows, :]
        outs[part][...] = total


def finish_kernel(*refs):
    ins, out_ref, turned = refs[:-2], refs[-2], refs[-1]
    total = ins[0][...]
    for other in ins[1:]:
        total = total + other[...]
    share, width = total.shape
    factor = lax.rsqrt(jnp.mean(total * total, axis=1, keepdims=True) + 1e-06)
    total = total * factor
    repeated = jnp.concatenate([total] * (LANES // share), axis=0)
    for group in range(width // LANES):
        turned[group * LANES : (group + 1) * LANES, :] = repeated[:, group * LANES : (group + 1) * LANES].T
    slab = lax.broadcasted_iota(jnp.int32, (SUBLANES, LANES), 1) // share
    features = width // out_ref.shape[0]
    slabs = features // SUBLANES
    for owner in range(out_ref.shape[0]):
        tile = turned[owner * features : owner * features + SUBLANES, :]
        for j in range(1, slabs):
            start = owner * features + j * SUBLANES
            tile = jnp.where(slab == j, turned[start : start + SUBLANES, :], tile)
        out_ref[owner] = tile


def place_kernel(tiles_ref, out_ref):
    owners = tiles_ref.shape[0]
    features, centroids = out_ref.shape
    share = centroids // owners
    per = LANES // share
    slab = lax.broadcasted_iota(jnp.int32, (SUBLANES, LANES), 1) // share
    for group in range(owners // per):
        for j in range(features // SUBLANES):
            made = None
            for s in range(per):
                tile = tiles_ref[group * per + s]
                shift = (share * (s - j)) % LANES
                moved = pltpu.roll(tile, shift, 1) if shift else tile
                made = moved if made is None else jnp.where(slab == s, moved, made)
            out_ref[j * SUBLANES : (j + 1) * SUBLANES, group * LANES : (group + 1) * LANES] = made


def ring(count, step):
    return [(i, (i + step) % count) for i in range(count)]


def per_device(sizes, embeddings, centroids):
    chips_y, chips_x, cores, clusters = sizes
    owners = chips_y * chips_x * cores
    rows, width = embeddings.shape
    local = centroids.shape[0]
    share = local // owners
    target = rows * owners / (local * clusters)
    order = share_order(chips_y, chips_x, share)
    f32, bf16 = jnp.float32, jnp.bfloat16
    chunk = 256

    kernel, unit_rows, columns = pl.pallas_call(
        functools.partial(prepare_kernel, order),
        grid=(rows // chunk,),
        in_specs=[
            pl.BlockSpec((chunk, width), lambda i: (i, 0)),
            pl.BlockSpec((local, width), lambda i: (0, 0)),
        ],
        out_specs=[VMEM, VMEM, VMEM],
        out_shape=[
            pltpu.VMEM((local, rows), f32),
            pltpu.VMEM((rows, width), bf16),
            pltpu.VMEM((owners, local // LANES, LANES), f32),
        ],
        scratch_shapes=[pltpu.VMEM((local, width), bf16), pltpu.VMEM((local, LANES), f32)],
        compiler_params=params(16),
        name="prepare",
    )(streamed(embeddings), streamed(centroids))

    def column_exchange(sums):
        return lax.all_to_all(sums, ROWS_DP, 0, 0)

    def row_exchange(sums):
        return lax.all_to_all(sums, "cluster", 0, 0)

    for sweep in range(SCALING_PASSES):
        if sweep:
            columns = pl.pallas_call(
                column_kernel,
                in_specs=[VMEM, VMEM],
                out_specs=VMEM,
                out_shape=pltpu.VMEM((owners, local // LANES, LANES), f32),
                scratch_shapes=[pltpu.VMEM((local, LANES), f32)],
                compiler_params=params(),
                name="columns",
            )(resident(row_sums), resident(kernel))
        columns = column_exchange(columns)
        row_sums = pl.pallas_call(
            functools.partial(row_kernel, target),
            in_specs=[VMEM, VMEM],
            out_specs=VMEM,
            out_shape=pltpu.VMEM((clusters, rows // LANES, LANES), f32),
            scratch_shapes=[pltpu.VMEM((local, LANES), f32)],
            compiler_params=params(),
            name="rows",
        )(resident(columns), resident(kernel))
        row_sums = row_exchange(row_sums)

    half = owners // cores * share

    def weighted(given, parts):
        return pl.pallas_call(
            functools.partial(sums_kernel, (chips_x, chips_y), given),
            in_specs=[VMEM] * 3,
            out_specs=[VMEM] * parts,
            out_shape=[pltpu.VMEM((half // parts, width), f32)] * parts,
            scratch_shapes=[pltpu.VMEM((half, rows), bf16)],
            compiler_params=params(8),
            cost_estimate=pl.CostEstimate(
                flops=2 * half * rows * width, bytes_accessed=4 * half * (rows + width), transcendentals=0
            ),
            name="sums",
        )(resident(row_sums), resident(kernel), resident(unit_rows))

    (given,) = weighted(True, 1)
    received = lax.ppermute(given, "core", ring(2, 1))
    kept = weighted(False, chips_x)

    first_parts = pl.pallas_call(
        functools.partial(add_kernel, chips_x),
        in_specs=[VMEM] * (1 + chips_x),
        out_specs=[VMEM] * chips_x,
        out_shape=[pltpu.VMEM((half // chips_x, width), f32)] * chips_x,
        compiler_params=params(),
        name="cores",
    )(resident(received), *[resident(part) for part in kept])

    def stage(parts, x_core):
        got = [parts[0]]
        for k in (1, 3, 2):
            pairs = []
            for j in range(chips_y):
                for i in range(chips_x):
                    for c in range(cores):
                        if c == x_core:
                            to = (j * chips_x + (i + k) % chips_x) * cores + c
                        else:
                            to = ((j + k) % chips_y * chips_x + i) * cores + c
                        pairs.append(((j * chips_x + i) * cores + c, to))
            got.append(lax.ppermute(parts[k], ROWS_DP, pairs))
        return got

    got = stage(first_parts, 0)
    second_parts = pl.pallas_call(
        functools.partial(fold_kernel, chips_y),
        in_specs=[VMEM] * len(got),
        out_specs=[VMEM] * chips_y,
        out_shape=[pltpu.VMEM((share, width), f32)] * chips_y,
        compiler_params=params(),
        name="fold",
    )(*[resident(part) for part in got])
    got = stage(second_parts, 1)
    tiles = pl.pallas_call(
        finish_kernel,
        in_specs=[VMEM] * len(got),
        out_specs=VMEM,
        out_shape=pltpu.VMEM((owners, SUBLANES, LANES), f32),
        scratch_shapes=[pltpu.VMEM((width, LANES), f32)],
        compiler_params=params(),
        name="finish",
    )(*[resident(part) for part in got])
    tiles = lax.all_to_all(tiles, ROWS_DP, 0, 0)
    placed = pl.pallas_call(
        place_kernel,
        in_specs=[VMEM],
        out_specs=VMEM,
        out_shape=jax.ShapeDtypeStruct((width // owners, local), f32),
        compiler_params=params(),
        name="place",
    )(resident(tiles))
    return placed.T


def solution(mesh):
    clusters = mesh.shape["cluster"]
    sizes = (4, 4, 2, clusters)
    split = Mesh(mesh.devices.reshape(sizes), ROWS_DP + ("cluster",))
    return jax.shard_map(
        functools.partial(per_device, sizes),
        mesh=split,
        in_specs=(P(ROWS_DP, None), P("cluster", None)),
        out_specs=P("cluster", ROWS_DP),
        check_vma=False,
    )
```

```python
import functools

import jax
import jax.numpy as jnp
from jax import lax
from jax.experimental import pallas as pl
from jax.experimental.pallas import tpu as pltpu
from jax.sharding import Mesh
from jax.sharding import PartitionSpec as P

SCALING_PASSES = 3
SOFTNESS_LEVEL = 0.025
LOG2_E = 1.4426950408889634
EXPONENT_SLOPE = LOG2_E / SOFTNESS_LEVEL
ROWS_DP = ("y", "x", "core")
LANES = 128
SUBLANES = 8

VMEM = pl.BlockSpec(memory_space=pltpu.VMEM)


def resident(array):
    return pltpu.with_memory_space_constraint(array, pltpu.VMEM)


def streamed(array):
    return pltpu.with_memory_space_constraint(array, pltpu.HBM)


def params(mebibytes=4):
    return pltpu.CompilerParams(vmem_limit_bytes=mebibytes * 1024 * 1024)


def unit(values):
    values = values.astype(jnp.float32)
    width = values.shape[1]
    factor = lax.rsqrt(jnp.mean(values * values, axis=1, keepdims=True) + 1e-06)
    return (values * factor * width ** (-0.5)).astype(jnp.bfloat16)


def share_order(chips_y, chips_x, share):
    order = []
    for x in range(chips_x):
        for y in range(chips_y):
            order.append((chips_x * y + x) * 2)
    for y in range(chips_y):
        for x in range(chips_x):
            order.append((chips_x * y + x) * 2 + 1)
    return order


def to_lanes(partial_ref, out_ref):
    copies = out_ref.shape[0]
    rows = []
    for group in range(partial_ref.shape[0] // LANES):
        block = partial_ref[group * LANES : (group + 1) * LANES, :]
        rows.append(jnp.sum(block.T, axis=0, keepdims=True))
    total = jnp.concatenate(rows, axis=0)
    for copy in range(copies):
        out_ref[copy] = total


def prepare_kernel(
    order, chunk, embeddings_ref, centroids_ref, kernel_ref, unit_ref, column_ref,
    raw_rows, raw_centroids, unit_centroids, even_rows, odd_rows, even_cosine, odd_cosine, partial, arrived,
):
    share = centroids_ref.shape[0] // len(order)
    chunks = embeddings_ref.shape[0] // chunk

    copies = [
        pltpu.make_async_copy(centroids_ref, raw_centroids, arrived.at[0]),
        pltpu.make_async_copy(embeddings_ref, raw_rows, arrived.at[1]),
    ]
    for copy in copies:
        copy.start()

    def normalise(index, out_ref):
        start = pl.multiple_of(index * chunk, chunk)
        rows = unit(raw_rows[pl.ds(start, chunk), :])
        out_ref[...] = rows
        unit_ref[pl.ds(start, chunk), :] = rows

    def product(rows_ref, out_ref):
        out_ref[...] = lax.dot_general(
            unit_centroids[...], rows_ref[...], (((1,), (1,)), ((), ())), preferred_element_type=jnp.float32
        )

    def exponential(index, cosine_ref):
        start = pl.multiple_of(index * chunk, chunk)
        affinity = jnp.exp2((cosine_ref[...] - 1.0) * EXPONENT_SLOPE)
        kernel_ref[:, pl.ds(start, chunk)] = affinity
        folded = affinity[:, :LANES]
        for tile in range(1, chunk // LANES):
            folded = folded + affinity[:, tile * LANES : (tile + 1) * LANES]
        partial[...] += folded

    copies[0].wait()
    for place, block in enumerate(order):
        unit_centroids[place * share : (place + 1) * share, :] = unit(
            raw_centroids[block * share : (block + 1) * share, :]
        )
    partial[...] = jnp.zeros_like(partial)
    copies[1].wait()
    normalise(0, even_rows)
    product(even_rows, even_cosine)
    normalise(1, odd_rows)

    def body(pair, carry):
        index = 2 * pair
        product(odd_rows, odd_cosine)
        exponential(index, even_cosine)
        normalise(index + 2, even_rows)
        product(even_rows, even_cosine)
        exponential(index + 1, odd_cosine)
        normalise(index + 3, odd_rows)
        return carry

    lax.fori_loop(0, chunks // 2 - 1, body, 0)
    product(odd_rows, odd_cosine)
    exponential(chunks - 2, even_cosine)
    exponential(chunks - 1, odd_cosine)
    to_lanes(partial, column_ref)


def row_kernel(target, columns_ref, kernel_ref, row_ref, scale_scratch):
    scale = target / jnp.sum(columns_ref[...], axis=0)
    for group in range(scale.shape[0]):
        scale_scratch[group * LANES : (group + 1) * LANES, :] = jnp.broadcast_to(
            scale[group : group + 1, :], (LANES, LANES)
        ).T
    centroids, rows = kernel_ref.shape
    tiles = rows // LANES
    height = 32

    def body(step, sums):
        start = pl.multiple_of(step * height, height)
        factor = scale_scratch[pl.ds(start, height), :]
        out = []
        for tile in range(tiles):
            product = kernel_ref[pl.ds(start, height), tile * LANES : (tile + 1) * LANES] * factor
            out.append(sums[tile] + jnp.sum(product.reshape(height // SUBLANES, SUBLANES, LANES), axis=0))
        return tuple(out)

    sums = lax.fori_loop(
        0, centroids // height, body, tuple(jnp.zeros((SUBLANES, LANES), jnp.float32) for _ in range(tiles))
    )
    total = jnp.concatenate([jnp.sum(tile, axis=0, keepdims=True) for tile in sums], axis=0)
    for copy in range(row_ref.shape[0]):
        row_ref[copy] = total


def column_kernel(rows_ref, kernel_ref, column_ref, partial):
    scale = 1.0 / jnp.sum(rows_ref[...], axis=0)
    centroids, rows = kernel_ref.shape
    tiles = rows // LANES
    height = 32
    factors = [jnp.broadcast_to(scale[tile : tile + 1, :], (SUBLANES, LANES)) for tile in range(tiles)]

    def body(step, carry):
        start = pl.multiple_of(step * height, height)
        total = None
        for tile in range(tiles):
            block = kernel_ref[pl.ds(start, height), tile * LANES : (tile + 1) * LANES]
            product = block.reshape(height // SUBLANES, SUBLANES, LANES) * factors[tile][None]
            total = product if total is None else total + product
        partial[pl.ds(start, height), :] = total.reshape(height, LANES)
        return carry

    lax.fori_loop(0, centroids // height, body, 0)
    to_lanes(partial, column_ref)


def weigh(kernel_ref, scale, weight_scratch, source, place, share):
    tiles = kernel_ref.shape[1] // LANES
    for tile in range(tiles):
        lanes = slice(tile * LANES, (tile + 1) * LANES)
        weight_scratch[place * share : (place + 1) * share, lanes] = (
            kernel_ref[pl.ds(source, share), lanes] * scale[tile : tile + 1, :]
        ).astype(jnp.bfloat16)


def sums_kernel(counts, given, distances, rows_ref, kernel_ref, unit_ref, *rest):
    received, outs, weight_scratch = rest[: -1 - len(distances)], rest[-1 - len(distances) : -1], rest[-1]
    slow, fast = counts
    half = slow * fast
    share = kernel_ref.shape[0] // (2 * half)
    scale = 1.0 / jnp.sum(rows_ref[...], axis=0)
    y, x, core = (lax.axis_index(name) for name in ROWS_DP)
    base = 1 - core if given else core
    first, second = jnp.where(base == 0, x, y), jnp.where(base == 0, y, x)
    height = fast * share
    for part, a in enumerate(distances):
        for b in range(fast):
            block = base * half + lax.rem(first + a, slow) * fast + lax.rem(second + b, fast)
            weigh(kernel_ref, scale, weight_scratch, pl.multiple_of(block * share, share), part * fast + b, share)
    for part in range(len(distances)):
        sums = jnp.dot(
            weight_scratch[part * height : (part + 1) * height, :], unit_ref[...], preferred_element_type=jnp.float32
        )
        outs[part][...] = sums + received[part][...] if received else sums


def fold_kernel(parts, *refs):
    ins, outs = refs[:-parts], refs[-parts:]
    share = outs[0].shape[0]
    for part in range(parts):
        rows = slice(part * share, (part + 1) * share)
        total = ins[0][rows, :]
        for other in ins[1:]:
            total = total + other[rows, :]
        outs[part][...] = total


def finish_kernel(*refs):
    ins, out_ref, turned = refs[:-2], refs[-2], refs[-1]
    total = ins[0][...]
    for other in ins[1:]:
        total = total + other[...]
    share, width = total.shape
    factor = lax.rsqrt(jnp.mean(total * total, axis=1, keepdims=True) + 1e-06)
    total = total * factor
    repeated = jnp.concatenate([total] * (LANES // share), axis=0)
    for group in range(width // LANES):
        turned[group * LANES : (group + 1) * LANES, :] = repeated[:, group * LANES : (group + 1) * LANES].T
    slab = lax.broadcasted_iota(jnp.int32, (SUBLANES, LANES), 1) // share
    features = width // out_ref.shape[0]
    slabs = features // SUBLANES
    for owner in range(out_ref.shape[0]):
        tile = turned[owner * features : owner * features + SUBLANES, :]
        for j in range(1, slabs):
            start = owner * features + j * SUBLANES
            tile = jnp.where(slab == j, turned[start : start + SUBLANES, :], tile)
        out_ref[owner] = tile


def place_kernel(tiles_ref, out_ref):
    owners = tiles_ref.shape[0]
    features, centroids = out_ref.shape
    share = centroids // owners
    per = LANES // share
    slab = lax.broadcasted_iota(jnp.int32, (SUBLANES, LANES), 1) // share
    for group in range(owners // per):
        for j in range(features // SUBLANES):
            made = None
            for s in range(per):
                tile = tiles_ref[group * per + s]
                shift = (share * (s - j)) % LANES
                moved = pltpu.roll(tile, shift, 1) if shift else tile
                made = moved if made is None else jnp.where(slab == s, moved, made)
            out_ref[j * SUBLANES : (j + 1) * SUBLANES, group * LANES : (group + 1) * LANES] = made


def ring(count, step):
    return [(i, (i + step) % count) for i in range(count)]


def per_device(sizes, embeddings, centroids):
    chips_y, chips_x, cores, clusters = sizes
    owners = chips_y * chips_x * cores
    rows, width = embeddings.shape
    local = centroids.shape[0]
    share = local // owners
    target = rows * owners / (local * clusters)
    order = share_order(chips_y, chips_x, share)
    f32, bf16 = jnp.float32, jnp.bfloat16
    chunk = 512

    kernel, unit_rows, columns = pl.pallas_call(
        functools.partial(prepare_kernel, order, chunk),
        in_specs=[pl.BlockSpec(memory_space=pltpu.HBM)] * 2,
        out_specs=[VMEM, VMEM, VMEM],
        out_shape=[
            pltpu.VMEM((local, rows), f32),
            pltpu.VMEM((rows, width), bf16),
            pltpu.VMEM((owners, local // LANES, LANES), f32),
        ],
        scratch_shapes=[
            pltpu.VMEM((rows, width), bf16),
            pltpu.VMEM((local, width), bf16),
            pltpu.VMEM((local, width), bf16),
            pltpu.VMEM((chunk, width), bf16),
            pltpu.VMEM((chunk, width), bf16),
            pltpu.VMEM((local, chunk), f32),
            pltpu.VMEM((local, chunk), f32),
            pltpu.VMEM((local, LANES), f32),
            pltpu.SemaphoreType.DMA((2,)),
        ],
        compiler_params=params(24),
        name="prepare",
    )(streamed(embeddings), streamed(centroids))

    def column_exchange(sums):
        return lax.all_to_all(sums, ROWS_DP, 0, 0)

    def row_exchange(sums):
        return lax.all_to_all(sums, "cluster", 0, 0)

    for sweep in range(SCALING_PASSES):
        if sweep:
            columns = pl.pallas_call(
                column_kernel,
                in_specs=[VMEM, VMEM],
                out_specs=VMEM,
                out_shape=pltpu.VMEM((owners, local // LANES, LANES), f32),
                scratch_shapes=[pltpu.VMEM((local, LANES), f32)],
                compiler_params=params(),
                name="columns",
            )(resident(row_sums), resident(kernel))
        columns = column_exchange(columns)
        row_sums = pl.pallas_call(
            functools.partial(row_kernel, target),
            in_specs=[VMEM, VMEM],
            out_specs=VMEM,
            out_shape=pltpu.VMEM((clusters, rows // LANES, LANES), f32),
            scratch_shapes=[pltpu.VMEM((local, LANES), f32)],
            compiler_params=params(),
            name="rows",
        )(resident(columns), resident(kernel))
        row_sums = row_exchange(row_sums)

    height = chips_y * share

    def weighted(row_sums, given, distances, received=()):
        count = len(distances)
        return pl.pallas_call(
            functools.partial(sums_kernel, (chips_x, chips_y), given, distances),
            in_specs=[VMEM] * (3 + len(received)),
            out_specs=[VMEM] * count,
            out_shape=[pltpu.VMEM((height, width), f32)] * count,
            scratch_shapes=[pltpu.VMEM((count * height, rows), bf16)],
            compiler_params=params(6),
            cost_estimate=pl.CostEstimate(
                flops=2 * count * height * rows * width,
                bytes_accessed=4 * count * height * (rows + width),
                transcendentals=0,
            ),
            name="sums",
        )(resident(row_sums), resident(kernel), resident(unit_rows), *[resident(part) for part in received])

    def swap(parts):
        return [lax.ppermute(part, "core", ring(2, 1)) for part in parts]

    def hop(part, k, x_core):
        pairs = []
        for j in range(chips_y):
            for i in range(chips_x):
                for c in range(cores):
                    if c == x_core:
                        to = (j * chips_x + (i + k) % chips_x) * cores + c
                    else:
                        to = ((j + k) % chips_y * chips_x + i) * cores + c
                    pairs.append(((j * chips_x + i) * cores + c, to))
        return lax.ppermute(part, ROWS_DP, pairs)

    def after(value, *others):
        return lax.optimization_barrier((value,) + others)[0]

    far = weighted(row_sums, True, (2,))
    row_sums = after(row_sums, *far)
    far = swap(far)
    near = weighted(row_sums, True, (1, 3))
    (part_2,) = weighted(row_sums, False, (2,), far)
    got_2 = hop(part_2, 2, 0)
    near = swap([after(part, part_2) for part in near])
    row_sums = after(row_sums, part_2)
    own = weighted(row_sums, True, (0,))
    part_1, part_3 = weighted(row_sums, False, (1, 3), near)
    got_1, got_3 = hop(part_1, 1, 0), hop(part_3, 3, 0)
    row_sums = after(row_sums, part_1)
    own = swap([after(part, part_1) for part in own])
    part_0 = weighted(row_sums, False, (0,))
    got = [*part_0, *own, got_2, got_1, got_3]
    second_parts = pl.pallas_call(
        functools.partial(fold_kernel, chips_y),
        in_specs=[VMEM] * len(got),
        out_specs=[VMEM] * chips_y,
        out_shape=[pltpu.VMEM((share, width), f32)] * chips_y,
        compiler_params=params(),
        name="fold",
    )(*[resident(part) for part in got])
    got = [second_parts[0]] + [hop(second_parts[k], k, 1) for k in (1, 3, 2)]
    tiles = pl.pallas_call(
        finish_kernel,
        in_specs=[VMEM] * len(got),
        out_specs=VMEM,
        out_shape=pltpu.VMEM((owners, SUBLANES, LANES), f32),
        scratch_shapes=[pltpu.VMEM((width, LANES), f32)],
        compiler_params=params(),
        name="finish",
    )(*[resident(part) for part in got])
    tiles = lax.all_to_all(tiles, ROWS_DP, 0, 0)
    placed = pl.pallas_call(
        place_kernel,
        in_specs=[VMEM],
        out_specs=VMEM,
        out_shape=jax.ShapeDtypeStruct((width // owners, local), f32),
        compiler_params=params(),
        name="place",
    )(resident(tiles))
    return placed.T


def solution(mesh):
    clusters = mesh.shape["cluster"]
    sizes = (4, 4, 2, clusters)
    split = Mesh(mesh.devices.reshape(sizes), ROWS_DP + ("cluster",))
    return jax.shard_map(
        functools.partial(per_device, sizes),
        mesh=split,
        in_specs=(P(ROWS_DP, None), P("cluster", None)),
        out_specs=P("cluster", ROWS_DP),
        check_vma=False,
    )
```

```python
import functools

import jax
import jax.numpy as jnp
from jax import lax
from jax.experimental import pallas as pl
from jax.experimental.pallas import tpu as pltpu
from jax.sharding import Mesh
from jax.sharding import PartitionSpec as P

SCALING_PASSES = 3
SOFTNESS_LEVEL = 0.025
LOG2_E = 1.4426950408889634
EXPONENT_SLOPE = LOG2_E / SOFTNESS_LEVEL
ROWS_DP = ("y", "x", "core")
LANES = 128
SUBLANES = 8

VMEM = pl.BlockSpec(memory_space=pltpu.VMEM)


def resident(array):
    return pltpu.with_memory_space_constraint(array, pltpu.VMEM)


def streamed(array):
    return pltpu.with_memory_space_constraint(array, pltpu.HBM)


def params(mebibytes=4):
    return pltpu.CompilerParams(vmem_limit_bytes=mebibytes * 1024 * 1024)


def unit(values):
    values = values.astype(jnp.float32)
    width = values.shape[1]
    factor = lax.rsqrt(jnp.mean(values * values, axis=1, keepdims=True) + 1e-06)
    return (values * factor * width ** (-0.5)).astype(jnp.bfloat16)


def share_order(chips_y, chips_x, share):
    order = []
    for x in range(chips_x):
        for y in range(chips_y):
            order.append((chips_x * y + x) * 2)
    for y in range(chips_y):
        for x in range(chips_x):
            order.append((chips_x * y + x) * 2 + 1)
    return order


def to_lanes(partial_ref, out_ref):
    copies = out_ref.shape[0]
    rows = []
    for group in range(partial_ref.shape[0] // LANES):
        block = partial_ref[group * LANES : (group + 1) * LANES, :]
        rows.append(jnp.sum(block.T, axis=0, keepdims=True))
    total = jnp.concatenate(rows, axis=0)
    for copy in range(copies):
        out_ref[copy] = total


def prepare_kernel(
    order, chunk, embeddings_ref, centroids_ref, kernel_ref, unit_ref, column_ref,
    raw_rows, raw_centroids, unit_centroids, even_rows, odd_rows, even_cosine, odd_cosine, partial, arrived,
):
    share = centroids_ref.shape[0] // len(order)
    chunks = embeddings_ref.shape[0] // chunk

    def fetch(start, size, which):
        rows = pl.ds(start, size)
        return pltpu.make_async_copy(embeddings_ref.at[rows, :], raw_rows.at[rows, :], arrived.at[which])

    fetch_centroids = pltpu.make_async_copy(centroids_ref, raw_centroids, arrived.at[0])
    fetch_first = fetch(0, chunk, 1)
    fetch_rest = fetch(chunk, embeddings_ref.shape[0] - chunk, 2)
    fetch_centroids.start()
    fetch_first.start()

    def normalise(index, out_ref):
        start = pl.multiple_of(index * chunk, chunk)
        rows = unit(raw_rows[pl.ds(start, chunk), :])
        out_ref[...] = rows
        unit_ref[pl.ds(start, chunk), :] = rows

    def product(rows_ref, out_ref):
        out_ref[...] = lax.dot_general(
            unit_centroids[...], rows_ref[...], (((1,), (1,)), ((), ())), preferred_element_type=jnp.float32
        )

    def exponential(index, cosine_ref):
        start = pl.multiple_of(index * chunk, chunk)
        affinity = jnp.exp2((cosine_ref[...] - 1.0) * EXPONENT_SLOPE)
        kernel_ref[:, pl.ds(start, chunk)] = affinity
        folded = affinity[:, :LANES]
        for tile in range(1, chunk // LANES):
            folded = folded + affinity[:, tile * LANES : (tile + 1) * LANES]
        partial[...] += folded

    fetch_centroids.wait()
    fetch_rest.start()
    for place, block in enumerate(order):
        unit_centroids[place * share : (place + 1) * share, :] = unit(
            raw_centroids[block * share : (block + 1) * share, :]
        )
    partial[...] = jnp.zeros_like(partial)
    fetch_first.wait()
    normalise(0, even_rows)
    product(even_rows, even_cosine)
    fetch_rest.wait()
    normalise(1, odd_rows)

    def body(pair, carry):
        index = 2 * pair
        product(odd_rows, odd_cosine)
        exponential(index, even_cosine)
        normalise(index + 2, even_rows)
        product(even_rows, even_cosine)
        exponential(index + 1, odd_cosine)
        normalise(index + 3, odd_rows)
        return carry

    lax.fori_loop(0, chunks // 2 - 1, body, 0)
    product(odd_rows, odd_cosine)
    exponential(chunks - 2, even_cosine)
    exponential(chunks - 1, odd_cosine)
    to_lanes(partial, column_ref)


def row_kernel(target, columns_ref, kernel_ref, row_ref, scale_scratch):
    scale = target / jnp.sum(columns_ref[...], axis=0)
    for group in range(scale.shape[0]):
        scale_scratch[group * LANES : (group + 1) * LANES, :] = jnp.broadcast_to(
            scale[group : group + 1, :], (LANES, LANES)
        ).T
    centroids, rows = kernel_ref.shape
    tiles = rows // LANES
    height = 32

    def body(step, sums):
        start = pl.multiple_of(step * height, height)
        factor = scale_scratch[pl.ds(start, height), :]
        out = []
        for tile in range(tiles):
            product = kernel_ref[pl.ds(start, height), tile * LANES : (tile + 1) * LANES] * factor
            out.append(sums[tile] + jnp.sum(product.reshape(height // SUBLANES, SUBLANES, LANES), axis=0))
        return tuple(out)

    nothing = tuple(jnp.zeros((SUBLANES, LANES), jnp.float32) for _ in range(tiles))
    sums = lax.fori_loop(0, centroids // height, body, nothing, unroll=8)
    total = jnp.concatenate([jnp.sum(tile, axis=0, keepdims=True) for tile in sums], axis=0)
    for copy in range(row_ref.shape[0]):
        row_ref[copy] = total


def column_kernel(rows_ref, kernel_ref, column_ref, partial):
    scale = 1.0 / jnp.sum(rows_ref[...], axis=0)
    centroids, rows = kernel_ref.shape
    tiles = rows // LANES
    height = 32
    factors = [jnp.broadcast_to(scale[tile : tile + 1, :], (SUBLANES, LANES)) for tile in range(tiles)]

    def body(step, carry):
        start = pl.multiple_of(step * height, height)
        total = None
        for tile in range(tiles):
            block = kernel_ref[pl.ds(start, height), tile * LANES : (tile + 1) * LANES]
            product = block.reshape(height // SUBLANES, SUBLANES, LANES) * factors[tile][None]
            total = product if total is None else total + product
        partial[pl.ds(start, height), :] = total.reshape(height, LANES)
        return carry

    lax.fori_loop(0, centroids // height, body, 0, unroll=8)
    to_lanes(partial, column_ref)


def weigh(kernel_ref, scale, weight_scratch, source, place, share):
    tiles = kernel_ref.shape[1] // LANES
    for tile in range(tiles):
        lanes = slice(tile * LANES, (tile + 1) * LANES)
        weight_scratch[place * share : (place + 1) * share, lanes] = (
            kernel_ref[pl.ds(source, share), lanes] * scale[tile : tile + 1, :]
        ).astype(jnp.bfloat16)


def sums_kernel(counts, given, distances, rows_ref, kernel_ref, unit_ref, *rest):
    received, (out_ref, weight_scratch) = rest[:-2], rest[-2:]
    slow, fast = counts
    half = slow * fast
    share = kernel_ref.shape[0] // (2 * half)
    scale = 1.0 / jnp.sum(rows_ref[...], axis=0)
    y, x, core = (lax.axis_index(name) for name in ROWS_DP)
    base = 1 - core if given else core
    first, second = jnp.where(base == 0, x, y), jnp.where(base == 0, y, x)
    for part, a in enumerate(distances):
        for b in range(fast):
            block = base * half + lax.rem(first + a, slow) * fast + lax.rem(second + b, fast)
            weigh(kernel_ref, scale, weight_scratch, pl.multiple_of(block * share, share), part * fast + b, share)
    height = 128
    for part in range(weight_scratch.shape[0] // height):
        rows = slice(part * height, (part + 1) * height)
        sums = jnp.dot(weight_scratch[rows, :], unit_ref[...], preferred_element_type=jnp.float32)
        out_ref[rows, :] = sums + received[0][rows, :] if received else sums


def add_kernel(own_ref, other_ref, *outs):
    height = outs[0].shape[0]
    for part, out_ref in enumerate(outs):
        rows = slice(part * height, (part + 1) * height)
        out_ref[...] = own_ref[rows, :] + other_ref[rows, :]


def fold_kernel(parts, *refs):
    ins, outs = refs[:-parts], refs[-parts:]
    share = outs[0].shape[0]
    for part in range(parts):
        rows = slice(part * share, (part + 1) * share)
        total = ins[0][rows, :]
        for other in ins[1:]:
            total = total + other[rows, :]
        outs[part][...] = total


def finish_kernel(*refs):
    ins, out_ref, turned = refs[:-2], refs[-2], refs[-1]
    total = ins[0][...]
    for other in ins[1:]:
        total = total + other[...]
    share, width = total.shape
    factor = lax.rsqrt(jnp.mean(total * total, axis=1, keepdims=True) + 1e-06)
    total = total * factor
    repeated = jnp.concatenate([total] * (LANES // share), axis=0)
    for group in range(width // LANES):
        turned[group * LANES : (group + 1) * LANES, :] = repeated[:, group * LANES : (group + 1) * LANES].T
    slab = lax.broadcasted_iota(jnp.int32, (SUBLANES, LANES), 1) // share
    features = width // out_ref.shape[0]
    slabs = features // SUBLANES
    for owner in range(out_ref.shape[0]):
        tile = turned[owner * features : owner * features + SUBLANES, :]
        for j in range(1, slabs):
            start = owner * features + j * SUBLANES
            tile = jnp.where(slab == j, turned[start : start + SUBLANES, :], tile)
        out_ref[owner] = tile


def place_kernel(tiles_ref, out_ref):
    owners = tiles_ref.shape[0]
    features, centroids = out_ref.shape
    share = centroids // owners
    per = LANES // share
    slab = lax.broadcasted_iota(jnp.int32, (SUBLANES, LANES), 1) // share
    for group in range(owners // per):
        for j in range(features // SUBLANES):
            made = None
            for s in range(per):
                tile = tiles_ref[group * per + s]
                shift = (share * (s - j)) % LANES
                moved = pltpu.roll(tile, shift, 1) if shift else tile
                made = moved if made is None else jnp.where(slab == s, moved, made)
            out_ref[j * SUBLANES : (j + 1) * SUBLANES, group * LANES : (group + 1) * LANES] = made


def ring(count, step):
    return [(i, (i + step) % count) for i in range(count)]


def per_device(sizes, embeddings, centroids):
    chips_y, chips_x, cores, clusters = sizes
    owners = chips_y * chips_x * cores
    rows, width = embeddings.shape
    local = centroids.shape[0]
    share = local // owners
    target = rows * owners / (local * clusters)
    order = share_order(chips_y, chips_x, share)
    f32, bf16 = jnp.float32, jnp.bfloat16
    chunk = 512

    kernel, unit_rows, columns = pl.pallas_call(
        functools.partial(prepare_kernel, order, chunk),
        in_specs=[pl.BlockSpec(memory_space=pltpu.HBM)] * 2,
        out_specs=[VMEM, VMEM, VMEM],
        out_shape=[
            pltpu.VMEM((local, rows), f32),
            pltpu.VMEM((rows, width), bf16),
            pltpu.VMEM((owners, local // LANES, LANES), f32),
        ],
        scratch_shapes=[
            pltpu.VMEM((rows, width), bf16),
            pltpu.VMEM((local, width), bf16),
            pltpu.VMEM((local, width), bf16),
            pltpu.VMEM((chunk, width), bf16),
            pltpu.VMEM((chunk, width), bf16),
            pltpu.VMEM((local, chunk), f32),
            pltpu.VMEM((local, chunk), f32),
            pltpu.VMEM((local, LANES), f32),
            pltpu.SemaphoreType.DMA((3,)),
        ],
        compiler_params=params(24),
        name="prepare",
    )(streamed(embeddings), streamed(centroids))

    def column_exchange(sums):
        return lax.all_to_all(sums, ROWS_DP, 0, 0)

    def row_exchange(sums):
        return lax.all_to_all(sums, "cluster", 0, 0)

    for sweep in range(SCALING_PASSES):
        if sweep:
            columns = pl.pallas_call(
                column_kernel,
                in_specs=[VMEM, VMEM],
                out_specs=VMEM,
                out_shape=pltpu.VMEM((owners, local // LANES, LANES), f32),
                scratch_shapes=[pltpu.VMEM((local, LANES), f32)],
                compiler_params=params(),
                name="columns",
            )(resident(row_sums), resident(kernel))
        columns = column_exchange(columns)
        row_sums = pl.pallas_call(
            functools.partial(row_kernel, target),
            in_specs=[VMEM, VMEM],
            out_specs=VMEM,
            out_shape=pltpu.VMEM((clusters, rows // LANES, LANES), f32),
            scratch_shapes=[pltpu.VMEM((local, LANES), f32)],
            compiler_params=params(),
            name="rows",
        )(resident(columns), resident(kernel))
        row_sums = row_exchange(row_sums)

    height = chips_y * share

    def weighted(row_sums, given, distances, *received):
        count = len(distances)
        return pl.pallas_call(
            functools.partial(sums_kernel, (chips_x, chips_y), given, distances),
            in_specs=[VMEM] * (3 + len(received)),
            out_specs=VMEM,
            out_shape=pltpu.VMEM((count * height, width), f32),
            scratch_shapes=[pltpu.VMEM((count * height, rows), bf16)],
            compiler_params=params(6),
            cost_estimate=pl.CostEstimate(
                flops=2 * count * height * rows * width,
                bytes_accessed=4 * count * height * (rows + width),
                transcendentals=0,
            ),
            name="sums",
        )(resident(row_sums), resident(kernel), resident(unit_rows), *[resident(part) for part in received])

    def add(body, name, shapes, *arrays):
        return pl.pallas_call(
            body,
            in_specs=[VMEM] * len(arrays),
            out_specs=[VMEM] * len(shapes),
            out_shape=[pltpu.VMEM(shape, f32) for shape in shapes],
            compiler_params=params(),
            name=name,
        )(*[resident(array) for array in arrays])

    def swap(part):
        return lax.ppermute(part, "core", ring(2, 1))

    def hop(part, k, x_core):
        pairs = []
        for j in range(chips_y):
            for i in range(chips_x):
                for c in range(cores):
                    if c == x_core:
                        to = (j * chips_x + (i + k) % chips_x) * cores + c
                    else:
                        to = ((j + k) % chips_y * chips_x + i) * cores + c
                    pairs.append(((j * chips_x + i) * cores + c, to))
        return lax.ppermute(part, ROWS_DP, pairs)

    def after(value, *others):
        return lax.optimization_barrier((value,) + others)[0]

    far = weighted(row_sums, True, (2,))
    row_sums = after(row_sums, far)
    far = swap(far)
    near = weighted(row_sums, True, (1, 3))
    row_sums = after(row_sums, near)
    far = weighted(row_sums, False, (2,), far)
    near = swap(after(near, far))
    row_sums = after(row_sums, far)
    far = hop(far, 2, 0)
    near_own = weighted(row_sums, False, (1, 3))
    up, down = add(add_kernel, "near", [(height, width)] * 2, near_own, near)
    row_sums = after(row_sums, up)
    up, down = hop(up, 1, 0), hop(down, 3, 0)
    own = weighted(row_sums, True, (0,))
    row_sums = after(row_sums, own)
    own = swap(own)
    part_0 = weighted(row_sums, False, (0,))
    second_parts = add(
        functools.partial(fold_kernel, chips_y), "fold", [(share, width)] * chips_y, part_0, own, far, up, down
    )
    got = [second_parts[0]] + [hop(second_parts[k], k, 1) for k in (1, 3, 2)]
    tiles = pl.pallas_call(
        finish_kernel,
        in_specs=[VMEM] * len(got),
        out_specs=VMEM,
        out_shape=pltpu.VMEM((owners, SUBLANES, LANES), f32),
        scratch_shapes=[pltpu.VMEM((width, LANES), f32)],
        compiler_params=params(),
        name="finish",
    )(*[resident(part) for part in got])
    tiles = lax.all_to_all(tiles, ROWS_DP, 0, 0)
    placed = pl.pallas_call(
        place_kernel,
        in_specs=[VMEM],
        out_specs=VMEM,
        out_shape=jax.ShapeDtypeStruct((width // owners, local), f32),
        compiler_params=params(),
        name="place",
    )(resident(tiles))
    return placed.T


def solution(mesh):
    clusters = mesh.shape["cluster"]
    sizes = (4, 4, 2, clusters)
    split = Mesh(mesh.devices.reshape(sizes), ROWS_DP + ("cluster",))
    return jax.shard_map(
        functools.partial(per_device, sizes),
        mesh=split,
        in_specs=(P(ROWS_DP, None), P("cluster", None)),
        out_specs=P("cluster", ROWS_DP),
        check_vma=False,
    )
```

```python
import functools

import jax
import jax.numpy as jnp
from jax import lax
from jax.experimental import pallas as pl
from jax.experimental.pallas import tpu as pltpu
from jax.sharding import Mesh
from jax.sharding import PartitionSpec as P

SCALING_PASSES = 3
SOFTNESS_LEVEL = 0.025
LOG2_E = 1.4426950408889634
EXPONENT_SLOPE = LOG2_E / SOFTNESS_LEVEL
ROWS_DP = ("y", "x", "core")
LANES = 128
SUBLANES = 8

VMEM = pl.BlockSpec(memory_space=pltpu.VMEM)


def resident(array):
    return pltpu.with_memory_space_constraint(array, pltpu.VMEM)


def streamed(array):
    return pltpu.with_memory_space_constraint(array, pltpu.HBM)


def params(mebibytes=4):
    return pltpu.CompilerParams(vmem_limit_bytes=mebibytes * 1024 * 1024)


def unit(values):
    values = values.astype(jnp.float32)
    width = values.shape[1]
    factor = lax.rsqrt(jnp.mean(values * values, axis=1, keepdims=True) + 1e-06)
    return (values * factor * width ** (-0.5)).astype(jnp.bfloat16)


def share_order(chips_y, chips_x, share):
    order = []
    for x in range(chips_x):
        for y in range(chips_y):
            order.append((chips_x * y + x) * 2)
    for y in range(chips_y):
        for x in range(chips_x):
            order.append((chips_x * y + x) * 2 + 1)
    return order


def to_lanes(partial_ref, out_ref):
    copies = out_ref.shape[0]
    rows = []
    for group in range(partial_ref.shape[0] // LANES):
        block = partial_ref[group * LANES : (group + 1) * LANES, :]
        rows.append(jnp.sum(block.T, axis=0, keepdims=True))
    total = jnp.concatenate(rows, axis=0)
    for copy in range(copies):
        out_ref[copy] = total


def prepare_kernel(
    order, chunk, embeddings_ref, centroids_ref, kernel_ref, unit_ref, column_ref,
    raw_rows, raw_centroids, unit_centroids, even_rows, odd_rows, even_cosine, odd_cosine, partial, arrived,
):
    share = centroids_ref.shape[0] // len(order)
    chunks = embeddings_ref.shape[0] // chunk

    def fetch(start, size, which):
        rows = pl.ds(start, size)
        return pltpu.make_async_copy(embeddings_ref.at[rows, :], raw_rows.at[rows, :], arrived.at[which])

    pieces = 4
    local = centroids_ref.shape[0]
    height = local // pieces
    fetch_centroids = []
    for piece in range(pieces):
        rows = pl.ds(piece * height, height)
        fetch_centroids.append(
            pltpu.make_async_copy(centroids_ref.at[rows, :], raw_centroids.at[rows, :], arrived.at[piece])
        )
    fetch_first = fetch(0, chunk, pieces)
    fetch_rest = fetch(chunk, embeddings_ref.shape[0] - chunk, pieces + 1)
    for copy in fetch_centroids:
        copy.start()
    fetch_first.start()
    fetch_rest.start()

    def normalise(index, out_ref):
        start = pl.multiple_of(index * chunk, chunk)
        rows = unit(raw_rows[pl.ds(start, chunk), :])
        out_ref[...] = rows
        unit_ref[pl.ds(start, chunk), :] = rows

    def product(rows_ref, out_ref):
        out_ref[...] = lax.dot_general(
            unit_centroids[...], rows_ref[...], (((1,), (1,)), ((), ())), preferred_element_type=jnp.float32
        )

    def exponential(index, cosine_ref):
        start = pl.multiple_of(index * chunk, chunk)
        affinity = jnp.exp2((cosine_ref[...] - 1.0) * EXPONENT_SLOPE)
        kernel_ref[:, pl.ds(start, chunk)] = affinity
        folded = affinity[:, :LANES]
        for tile in range(1, chunk // LANES):
            folded = folded + affinity[:, tile * LANES : (tile + 1) * LANES]
        partial[...] += folded

    for piece in range(pieces):
        fetch_centroids[piece].wait()
        for place, block in enumerate(order):
            if block * share // height == piece:
                unit_centroids[place * share : (place + 1) * share, :] = unit(
                    raw_centroids[block * share : (block + 1) * share, :]
                )
    partial[...] = jnp.zeros_like(partial)
    fetch_first.wait()
    normalise(0, even_rows)
    product(even_rows, even_cosine)
    fetch_rest.wait()
    normalise(1, odd_rows)

    def body(pair, carry):
        index = 2 * pair
        product(odd_rows, odd_cosine)
        exponential(index, even_cosine)
        normalise(index + 2, even_rows)
        product(even_rows, even_cosine)
        exponential(index + 1, odd_cosine)
        normalise(index + 3, odd_rows)
        return carry

    lax.fori_loop(0, chunks // 2 - 1, body, 0)
    product(odd_rows, odd_cosine)
    exponential(chunks - 2, even_cosine)
    exponential(chunks - 1, odd_cosine)
    to_lanes(partial, column_ref)


def row_kernel(target, columns_ref, kernel_ref, row_ref, scale_scratch):
    scale = target / jnp.sum(columns_ref[...], axis=0)
    for group in range(scale.shape[0]):
        scale_scratch[group * LANES : (group + 1) * LANES, :] = jnp.broadcast_to(
            scale[group : group + 1, :], (LANES, LANES)
        ).T
    centroids, rows = kernel_ref.shape
    tiles = rows // LANES
    height = 32

    def body(step, sums):
        start = pl.multiple_of(step * height, height)
        factor = scale_scratch[pl.ds(start, height), :]
        out = []
        for tile in range(tiles):
            product = kernel_ref[pl.ds(start, height), tile * LANES : (tile + 1) * LANES] * factor
            out.append(sums[tile] + jnp.sum(product.reshape(height // SUBLANES, SUBLANES, LANES), axis=0))
        return tuple(out)

    nothing = tuple(jnp.zeros((SUBLANES, LANES), jnp.float32) for _ in range(tiles))
    sums = lax.fori_loop(0, centroids // height, body, nothing, unroll=8)
    total = jnp.concatenate([jnp.sum(tile, axis=0, keepdims=True) for tile in sums], axis=0)
    for copy in range(row_ref.shape[0]):
        row_ref[copy] = total


def column_kernel(rows_ref, kernel_ref, column_ref, partial):
    scale = 1.0 / jnp.sum(rows_ref[...], axis=0)
    centroids, rows = kernel_ref.shape
    tiles = rows // LANES
    height = 32
    factors = [jnp.broadcast_to(scale[tile : tile + 1, :], (SUBLANES, LANES)) for tile in range(tiles)]

    def body(step, carry):
        start = pl.multiple_of(step * height, height)
        total = None
        for tile in range(tiles):
            block = kernel_ref[pl.ds(start, height), tile * LANES : (tile + 1) * LANES]
            product = block.reshape(height // SUBLANES, SUBLANES, LANES) * factors[tile][None]
            total = product if total is None else total + product
        partial[pl.ds(start, height), :] = total.reshape(height, LANES)
        return carry

    lax.fori_loop(0, centroids // height, body, 0, unroll=8)
    to_lanes(partial, column_ref)


def weigh(kernel_ref, scale, weight_scratch, source, place, share):
    tiles = kernel_ref.shape[1] // LANES
    for tile in range(tiles):
        lanes = slice(tile * LANES, (tile + 1) * LANES)
        weight_scratch[place * share : (place + 1) * share, lanes] = (
            kernel_ref[pl.ds(source, share), lanes] * scale[tile : tile + 1, :]
        ).astype(jnp.bfloat16)


def sums_kernel(counts, given, distances, rows_ref, kernel_ref, unit_ref, *rest):
    received, (out_ref, weight_scratch) = rest[:-2], rest[-2:]
    slow, fast = counts
    half = slow * fast
    share = kernel_ref.shape[0] // (2 * half)
    scale = 1.0 / jnp.sum(rows_ref[...], axis=0)
    y, x, core = (lax.axis_index(name) for name in ROWS_DP)
    base = 1 - core if given else core
    first, second = jnp.where(base == 0, x, y), jnp.where(base == 0, y, x)
    for part, a in enumerate(distances):
        for b in range(fast):
            block = base * half + lax.rem(first + a, slow) * fast + lax.rem(second + b, fast)
            weigh(kernel_ref, scale, weight_scratch, pl.multiple_of(block * share, share), part * fast + b, share)
    height = 128
    for part in range(weight_scratch.shape[0] // height):
        rows = slice(part * height, (part + 1) * height)
        sums = jnp.dot(weight_scratch[rows, :], unit_ref[...], preferred_element_type=jnp.float32)
        out_ref[rows, :] = sums + received[0][rows, :] if received else sums


def add_kernel(own_ref, other_ref, *outs):
    height = outs[0].shape[0]
    for part, out_ref in enumerate(outs):
        rows = slice(part * height, (part + 1) * height)
        out_ref[...] = own_ref[rows, :] + other_ref[rows, :]


def fold_kernel(parts, *refs):
    ins, outs = refs[:-parts], refs[-parts:]
    share = outs[0].shape[0]
    for part in range(parts):
        rows = slice(part * share, (part + 1) * share)
        total = ins[0][rows, :]
        for other in ins[1:]:
            total = total + other[rows, :]
        outs[part][...] = total


def finish_kernel(*refs):
    ins, out_ref, turned = refs[:-2], refs[-2], refs[-1]
    total = ins[0][...]
    for other in ins[1:]:
        total = total + other[...]
    share, width = total.shape
    factor = lax.rsqrt(jnp.mean(total * total, axis=1, keepdims=True) + 1e-06)
    total = total * factor
    repeated = jnp.concatenate([total] * (LANES // share), axis=0)
    for group in range(width // LANES):
        turned[group * LANES : (group + 1) * LANES, :] = repeated[:, group * LANES : (group + 1) * LANES].T
    slab = lax.broadcasted_iota(jnp.int32, (SUBLANES, LANES), 1) // share
    features = width // out_ref.shape[0]
    slabs = features // SUBLANES
    for owner in range(out_ref.shape[0]):
        tile = turned[owner * features : owner * features + SUBLANES, :]
        for j in range(1, slabs):
            start = owner * features + j * SUBLANES
            tile = jnp.where(slab == j, turned[start : start + SUBLANES, :], tile)
        out_ref[owner] = tile


def place_kernel(tiles_ref, out_ref):
    owners = tiles_ref.shape[0]
    features, centroids = out_ref.shape
    share = centroids // owners
    per = LANES // share
    slab = lax.broadcasted_iota(jnp.int32, (SUBLANES, LANES), 1) // share
    for group in range(owners // per):
        for j in range(features // SUBLANES):
            made = None
            for s in range(per):
                tile = tiles_ref[group * per + s]
                shift = (share * (s - j)) % LANES
                moved = pltpu.roll(tile, shift, 1) if shift else tile
                made = moved if made is None else jnp.where(slab == s, moved, made)
            out_ref[j * SUBLANES : (j + 1) * SUBLANES, group * LANES : (group + 1) * LANES] = made


def ring(count, step):
    return [(i, (i + step) % count) for i in range(count)]


def per_device(sizes, embeddings, centroids):
    chips_y, chips_x, cores, clusters = sizes
    owners = chips_y * chips_x * cores
    rows, width = embeddings.shape
    local = centroids.shape[0]
    share = local // owners
    target = rows * owners / (local * clusters)
    order = share_order(chips_y, chips_x, share)
    f32, bf16 = jnp.float32, jnp.bfloat16
    chunk = 512

    kernel, unit_rows, columns = pl.pallas_call(
        functools.partial(prepare_kernel, order, chunk),
        in_specs=[pl.BlockSpec(memory_space=pltpu.HBM)] * 2,
        out_specs=[VMEM, VMEM, VMEM],
        out_shape=[
            pltpu.VMEM((local, rows), f32),
            pltpu.VMEM((rows, width), bf16),
            pltpu.VMEM((owners, local // LANES, LANES), f32),
        ],
        scratch_shapes=[
            pltpu.VMEM((rows, width), bf16),
            pltpu.VMEM((local, width), bf16),
            pltpu.VMEM((local, width), bf16),
            pltpu.VMEM((chunk, width), bf16),
            pltpu.VMEM((chunk, width), bf16),
            pltpu.VMEM((local, chunk), f32),
            pltpu.VMEM((local, chunk), f32),
            pltpu.VMEM((local, LANES), f32),
            pltpu.SemaphoreType.DMA((6,)),
        ],
        compiler_params=params(24),
        name="prepare",
    )(streamed(embeddings), streamed(centroids))

    def column_exchange(sums):
        return lax.all_to_all(sums, ROWS_DP, 0, 0)

    def row_exchange(sums):
        return lax.all_to_all(sums, "cluster", 0, 0)

    for sweep in range(SCALING_PASSES):
        if sweep:
            columns = pl.pallas_call(
                column_kernel,
                in_specs=[VMEM, VMEM],
                out_specs=VMEM,
                out_shape=pltpu.VMEM((owners, local // LANES, LANES), f32),
                scratch_shapes=[pltpu.VMEM((local, LANES), f32)],
                compiler_params=params(),
                name="columns",
            )(resident(row_sums), resident(kernel))
        columns = column_exchange(columns)
        row_sums = pl.pallas_call(
            functools.partial(row_kernel, target),
            in_specs=[VMEM, VMEM],
            out_specs=VMEM,
            out_shape=pltpu.VMEM((clusters, rows // LANES, LANES), f32),
            scratch_shapes=[pltpu.VMEM((local, LANES), f32)],
            compiler_params=params(),
            name="rows",
        )(resident(columns), resident(kernel))
        row_sums = row_exchange(row_sums)

    height = chips_y * share

    def weighted(row_sums, given, distances, *received):
        count = len(distances)
        return pl.pallas_call(
            functools.partial(sums_kernel, (chips_x, chips_y), given, distances),
            in_specs=[VMEM] * (3 + len(received)),
            out_specs=VMEM,
            out_shape=pltpu.VMEM((count * height, width), f32),
            scratch_shapes=[pltpu.VMEM((count * height, rows), bf16)],
            compiler_params=params(6),
            cost_estimate=pl.CostEstimate(
                flops=2 * count * height * rows * width,
                bytes_accessed=4 * count * height * (rows + width),
                transcendentals=0,
            ),
            name="sums",
        )(resident(row_sums), resident(kernel), resident(unit_rows), *[resident(part) for part in received])

    def add(body, name, shapes, *arrays):
        return pl.pallas_call(
            body,
            in_specs=[VMEM] * len(arrays),
            out_specs=[VMEM] * len(shapes),
            out_shape=[pltpu.VMEM(shape, f32) for shape in shapes],
            compiler_params=params(),
            name=name,
        )(*[resident(array) for array in arrays])

    def swap(part):
        return lax.ppermute(part, "core", ring(2, 1))

    def hop(part, k, x_core):
        pairs = []
        for j in range(chips_y):
            for i in range(chips_x):
                for c in range(cores):
                    if c == x_core:
                        to = (j * chips_x + (i + k) % chips_x) * cores + c
                    else:
                        to = ((j + k) % chips_y * chips_x + i) * cores + c
                    pairs.append(((j * chips_x + i) * cores + c, to))
        return lax.ppermute(part, ROWS_DP, pairs)

    def after(value, *others):
        return lax.optimization_barrier((value,) + others)[0]

    far = weighted(row_sums, True, (2,))
    row_sums = after(row_sums, far)
    far = swap(far)
    near = weighted(row_sums, True, (1, 3))
    row_sums = after(row_sums, near)
    far = weighted(row_sums, False, (2,), far)
    near = swap(after(near, far))
    row_sums = after(row_sums, far)
    far = hop(far, 2, 0)
    near_own = weighted(row_sums, False, (1, 3))
    up, down = add(add_kernel, "near", [(height, width)] * 2, near_own, near)
    row_sums = after(row_sums, up)
    up, down = hop(up, 1, 0), hop(down, 3, 0)
    own = weighted(row_sums, True, (0,))
    row_sums = after(row_sums, own)
    own = swap(own)
    part_0 = weighted(row_sums, False, (0,))
    second_parts = add(
        functools.partial(fold_kernel, chips_y), "fold", [(share, width)] * chips_y, part_0, own, far, up, down
    )
    got = [second_parts[0]] + [hop(second_parts[k], k, 1) for k in (2, 3, 1)]
    tiles = pl.pallas_call(
        finish_kernel,
        in_specs=[VMEM] * len(got),
        out_specs=VMEM,
        out_shape=pltpu.VMEM((owners, SUBLANES, LANES), f32),
        scratch_shapes=[pltpu.VMEM((width, LANES), f32)],
        compiler_params=params(),
        name="finish",
    )(*[resident(part) for part in got])
    tiles = lax.all_to_all(tiles, ROWS_DP, 0, 0)
    placed = pl.pallas_call(
        place_kernel,
        in_specs=[VMEM],
        out_specs=VMEM,
        out_shape=jax.ShapeDtypeStruct((width // owners, local), f32),
        compiler_params=params(),
        name="place",
    )(resident(tiles))
    return placed.T


def solution(mesh):
    clusters = mesh.shape["cluster"]
    sizes = (4, 4, 2, clusters)
    split = Mesh(mesh.devices.reshape(sizes), ROWS_DP + ("cluster",))
    return jax.shard_map(
        functools.partial(per_device, sizes),
        mesh=split,
        in_specs=(P(ROWS_DP, None), P("cluster", None)),
        out_specs=P("cluster", ROWS_DP),
        check_vma=False,
    )
```

```python
import functools

import jax
import jax.numpy as jnp
from jax import lax
from jax.experimental import pallas as pl
from jax.experimental.pallas import tpu as pltpu
from jax.sharding import Mesh
from jax.sharding import PartitionSpec as P

SCALING_PASSES = 3
SOFTNESS_LEVEL = 0.025
LOG2_E = 1.4426950408889634
EXPONENT_SLOPE = LOG2_E / SOFTNESS_LEVEL
ROWS_DP = ("y", "x", "core")
LANES = 128
SUBLANES = 8

VMEM = pl.BlockSpec(memory_space=pltpu.VMEM)


def resident(array):
    return pltpu.with_memory_space_constraint(array, pltpu.VMEM)


def streamed(array):
    return pltpu.with_memory_space_constraint(array, pltpu.HBM)


def params(mebibytes=4):
    return pltpu.CompilerParams(vmem_limit_bytes=mebibytes * 1024 * 1024)


def unit(values):
    values = values.astype(jnp.float32)
    width = values.shape[1]
    factor = lax.rsqrt(jnp.mean(values * values, axis=1, keepdims=True) + 1e-06)
    return (values * factor * width ** (-0.5)).astype(jnp.bfloat16)


def share_order(chips_y, chips_x, share):
    order = []
    for x in range(chips_x):
        for y in range(chips_y):
            order.append((chips_x * y + x) * 2)
    for y in range(chips_y):
        for x in range(chips_x):
            order.append((chips_x * y + x) * 2 + 1)
    return order


def to_lanes(partial_ref, out_ref):
    copies = out_ref.shape[0]
    rows = []
    for group in range(partial_ref.shape[0] // LANES):
        block = partial_ref[group * LANES : (group + 1) * LANES, :]
        rows.append(jnp.sum(block.T, axis=0, keepdims=True))
    total = jnp.concatenate(rows, axis=0)
    for copy in range(copies):
        out_ref[copy] = total


def prepare_kernel(
    order, chunk, embeddings_ref, centroids_ref, kernel_ref, unit_ref, column_ref,
    raw_rows, raw_centroids, unit_centroids, even_rows, odd_rows, even_cosine, odd_cosine, partial, arrived,
):
    share = centroids_ref.shape[0] // len(order)
    chunks = embeddings_ref.shape[0] // chunk

    def fetch(start, size, which):
        rows = pl.ds(start, size)
        return pltpu.make_async_copy(embeddings_ref.at[rows, :], raw_rows.at[rows, :], arrived.at[which])

    pieces = 4
    local = centroids_ref.shape[0]
    height = local // pieces
    fetch_centroids = []
    for piece in range(pieces):
        rows = pl.ds(piece * height, height)
        fetch_centroids.append(
            pltpu.make_async_copy(centroids_ref.at[rows, :], raw_centroids.at[rows, :], arrived.at[piece])
        )
    fetch_first = fetch(0, chunk, pieces)
    fetch_rest = fetch(chunk, embeddings_ref.shape[0] - chunk, pieces + 1)
    for copy in fetch_centroids:
        copy.start()
    fetch_first.start()
    fetch_rest.start()

    def normalise(index, out_ref):
        start = pl.multiple_of(index * chunk, chunk)
        rows = unit(raw_rows[pl.ds(start, chunk), :])
        out_ref[...] = rows
        unit_ref[pl.ds(start, chunk), :] = rows

    def product(rows_ref, out_ref):
        out_ref[...] = lax.dot_general(
            unit_centroids[...], rows_ref[...], (((1,), (1,)), ((), ())), preferred_element_type=jnp.float32
        )

    def exponential(index, cosine_ref):
        start = pl.multiple_of(index * chunk, chunk)
        affinity = jnp.exp2((cosine_ref[...] - 1.0) * EXPONENT_SLOPE)
        kernel_ref[:, pl.ds(start, chunk)] = affinity
        folded = affinity[:, :LANES]
        for tile in range(1, chunk // LANES):
            folded = folded + affinity[:, tile * LANES : (tile + 1) * LANES]
        partial[...] += folded

    for piece in range(pieces):
        fetch_centroids[piece].wait()
        for place, block in enumerate(order):
            if block * share // height == piece:
                unit_centroids[place * share : (place + 1) * share, :] = unit(
                    raw_centroids[block * share : (block + 1) * share, :]
                )
    partial[...] = jnp.zeros_like(partial)
    fetch_first.wait()
    normalise(0, even_rows)
    product(even_rows, even_cosine)
    fetch_rest.wait()
    normalise(1, odd_rows)

    def body(pair, carry):
        index = 2 * pair
        product(odd_rows, odd_cosine)
        exponential(index, even_cosine)
        normalise(index + 2, even_rows)
        product(even_rows, even_cosine)
        exponential(index + 1, odd_cosine)
        normalise(index + 3, odd_rows)
        return carry

    lax.fori_loop(0, chunks // 2 - 1, body, 0)
    product(odd_rows, odd_cosine)
    exponential(chunks - 2, even_cosine)
    exponential(chunks - 1, odd_cosine)
    to_lanes(partial, column_ref)


def row_kernel(target, columns_ref, kernel_ref, row_ref, scale_scratch):
    scale = target / jnp.sum(columns_ref[...], axis=0)
    for group in range(scale.shape[0]):
        scale_scratch[group * LANES : (group + 1) * LANES, :] = jnp.broadcast_to(
            scale[group : group + 1, :], (LANES, LANES)
        ).T
    centroids, rows = kernel_ref.shape
    tiles = rows // LANES
    height = 32

    def body(step, sums):
        start = pl.multiple_of(step * height, height)
        factor = scale_scratch[pl.ds(start, height), :]
        out = []
        for tile in range(tiles):
            product = kernel_ref[pl.ds(start, height), tile * LANES : (tile + 1) * LANES] * factor
            out.append(sums[tile] + jnp.sum(product.reshape(height // SUBLANES, SUBLANES, LANES), axis=0))
        return tuple(out)

    nothing = tuple(jnp.zeros((SUBLANES, LANES), jnp.float32) for _ in range(tiles))
    sums = lax.fori_loop(0, centroids // height, body, nothing, unroll=8)
    total = jnp.concatenate([jnp.sum(tile, axis=0, keepdims=True) for tile in sums], axis=0)
    for copy in range(row_ref.shape[0]):
        row_ref[copy] = total


def column_kernel(rows_ref, kernel_ref, column_ref, partial):
    scale = 1.0 / jnp.sum(rows_ref[...], axis=0)
    centroids, rows = kernel_ref.shape
    tiles = rows // LANES
    height = 32
    factors = [jnp.broadcast_to(scale[tile : tile + 1, :], (SUBLANES, LANES)) for tile in range(tiles)]

    def body(step, carry):
        start = pl.multiple_of(step * height, height)
        total = None
        for tile in range(tiles):
            block = kernel_ref[pl.ds(start, height), tile * LANES : (tile + 1) * LANES]
            product = block.reshape(height // SUBLANES, SUBLANES, LANES) * factors[tile][None]
            total = product if total is None else total + product
        partial[pl.ds(start, height), :] = total.reshape(height, LANES)
        return carry

    lax.fori_loop(0, centroids // height, body, 0, unroll=8)
    to_lanes(partial, column_ref)


def weigh(kernel_ref, scale, weight_scratch, source, place, share):
    tiles = kernel_ref.shape[1] // LANES
    for tile in range(tiles):
        lanes = slice(tile * LANES, (tile + 1) * LANES)
        weight_scratch[place * share : (place + 1) * share, lanes] = (
            kernel_ref[pl.ds(source, share), lanes] * scale[tile : tile + 1, :]
        ).astype(jnp.bfloat16)


def sums_kernel(counts, blocks, rows_ref, kernel_ref, unit_ref, *rest):
    outs, weight_scratch = rest[:-1], rest[-1]
    slow, fast = counts
    half = slow * fast
    share = kernel_ref.shape[0] // (2 * half)
    scale = 1.0 / jnp.sum(rows_ref[...], axis=0)
    y, x, core = (lax.axis_index(name) for name in ROWS_DP)
    for part, (other, a) in enumerate(blocks):
        base = 1 - core if other else core
        first, second = jnp.where(base == 0, x, y), jnp.where(base == 0, y, x)
        for b in range(fast):
            block = base * half + lax.rem(first + a, slow) * fast + lax.rem(second + b, fast)
            weigh(kernel_ref, scale, weight_scratch, pl.multiple_of(block * share, share), part * fast + b, share)
    height = fast * share
    sums = jnp.dot(weight_scratch[...], unit_ref[...], preferred_element_type=jnp.float32)
    start = 0
    for out_ref in outs:
        out_ref[...] = sums[start : start + out_ref.shape[0], :]
        start += out_ref.shape[0]


def add_kernel(own_ref, other_ref, *outs):
    height = outs[0].shape[0]
    for part, out_ref in enumerate(outs):
        rows = slice(part * height, (part + 1) * height)
        out_ref[...] = own_ref[rows, :] + other_ref[rows, :]


def fold_kernel(parts, *refs):
    ins, outs = refs[:-parts], refs[-parts:]
    share = outs[0].shape[0]
    for part in range(parts):
        rows = slice(part * share, (part + 1) * share)
        total = ins[0][rows, :]
        for other in ins[1:]:
            total = total + other[rows, :]
        outs[part][...] = total


def finish_kernel(*refs):
    ins, out_ref, turned = refs[:-2], refs[-2], refs[-1]
    total = ins[0][...]
    for other in ins[1:]:
        total = total + other[...]
    share, width = total.shape
    factor = lax.rsqrt(jnp.mean(total * total, axis=1, keepdims=True) + 1e-06)
    total = total * factor
    repeated = jnp.concatenate([total] * (LANES // share), axis=0)
    for group in range(width // LANES):
        turned[group * LANES : (group + 1) * LANES, :] = repeated[:, group * LANES : (group + 1) * LANES].T
    slab = lax.broadcasted_iota(jnp.int32, (SUBLANES, LANES), 1) // share
    features = width // out_ref.shape[0]
    slabs = features // SUBLANES
    for owner in range(out_ref.shape[0]):
        tile = turned[owner * features : owner * features + SUBLANES, :]
        for j in range(1, slabs):
            start = owner * features + j * SUBLANES
            tile = jnp.where(slab == j, turned[start : start + SUBLANES, :], tile)
        out_ref[owner] = tile


def place_kernel(tiles_ref, out_ref):
    owners = tiles_ref.shape[0]
    features, centroids = out_ref.shape
    share = centroids // owners
    per = LANES // share
    slab = lax.broadcasted_iota(jnp.int32, (SUBLANES, LANES), 1) // share
    for group in range(owners // per):
        for j in range(features // SUBLANES):
            made = None
            for s in range(per):
                tile = tiles_ref[group * per + s]
                shift = (share * (s - j)) % LANES
                moved = pltpu.roll(tile, shift, 1) if shift else tile
                made = moved if made is None else jnp.where(slab == s, moved, made)
            out_ref[j * SUBLANES : (j + 1) * SUBLANES, group * LANES : (group + 1) * LANES] = made


def ring(count, step):
    return [(i, (i + step) % count) for i in range(count)]


def per_device(sizes, embeddings, centroids):
    chips_y, chips_x, cores, clusters = sizes
    owners = chips_y * chips_x * cores
    rows, width = embeddings.shape
    local = centroids.shape[0]
    share = local // owners
    target = rows * owners / (local * clusters)
    order = share_order(chips_y, chips_x, share)
    f32, bf16 = jnp.float32, jnp.bfloat16
    chunk = 512

    kernel, unit_rows, columns = pl.pallas_call(
        functools.partial(prepare_kernel, order, chunk),
        in_specs=[pl.BlockSpec(memory_space=pltpu.HBM)] * 2,
        out_specs=[VMEM, VMEM, VMEM],
        out_shape=[
            pltpu.VMEM((local, rows), f32),
            pltpu.VMEM((rows, width), bf16),
            pltpu.VMEM((owners, local // LANES, LANES), f32),
        ],
        scratch_shapes=[
            pltpu.VMEM((rows, width), bf16),
            pltpu.VMEM((local, width), bf16),
            pltpu.VMEM((local, width), bf16),
            pltpu.VMEM((chunk, width), bf16),
            pltpu.VMEM((chunk, width), bf16),
            pltpu.VMEM((local, chunk), f32),
            pltpu.VMEM((local, chunk), f32),
            pltpu.VMEM((local, LANES), f32),
            pltpu.SemaphoreType.DMA((6,)),
        ],
        compiler_params=params(24),
        name="prepare",
    )(streamed(embeddings), streamed(centroids))

    def column_exchange(sums):
        return lax.all_to_all(sums, ROWS_DP, 0, 0)

    def row_exchange(sums):
        return lax.all_to_all(sums, "cluster", 0, 0)

    for sweep in range(SCALING_PASSES):
        if sweep:
            columns = pl.pallas_call(
                column_kernel,
                in_specs=[VMEM, VMEM],
                out_specs=VMEM,
                out_shape=pltpu.VMEM((owners, local // LANES, LANES), f32),
                scratch_shapes=[pltpu.VMEM((local, LANES), f32)],
                compiler_params=params(),
                name="columns",
            )(resident(row_sums), resident(kernel))
        columns = column_exchange(columns)
        row_sums = pl.pallas_call(
            functools.partial(row_kernel, target),
            in_specs=[VMEM, VMEM],
            out_specs=VMEM,
            out_shape=pltpu.VMEM((clusters, rows // LANES, LANES), f32),
            scratch_shapes=[pltpu.VMEM((local, LANES), f32)],
            compiler_params=params(),
            name="rows",
        )(resident(columns), resident(kernel))
        row_sums = row_exchange(row_sums)

    height = chips_y * share

    def weighted(row_sums, *groups):
        blocks = [block for group in groups for block in group]
        count = len(blocks)
        return pl.pallas_call(
            functools.partial(sums_kernel, (chips_x, chips_y), blocks),
            in_specs=[VMEM] * 3,
            out_specs=[VMEM] * len(groups),
            out_shape=[pltpu.VMEM((len(group) * height, width), f32) for group in groups],
            scratch_shapes=[pltpu.VMEM((count * height, rows), bf16)],
            compiler_params=params(6),
            cost_estimate=pl.CostEstimate(
                flops=2 * count * height * rows * width,
                bytes_accessed=4 * count * height * (rows + width),
                transcendentals=0,
            ),
            name="sums",
        )(resident(row_sums), resident(kernel), resident(unit_rows))

    def add(body, name, shapes, *arrays):
        return pl.pallas_call(
            body,
            in_specs=[VMEM] * len(arrays),
            out_specs=[VMEM] * len(shapes),
            out_shape=[pltpu.VMEM(shape, f32) for shape in shapes],
            compiler_params=params(),
            name=name,
        )(*[resident(array) for array in arrays])

    def swap(part):
        return lax.ppermute(part, "core", ring(2, 1))

    def hop(part, k, x_core):
        pairs = []
        for j in range(chips_y):
            for i in range(chips_x):
                for c in range(cores):
                    if c == x_core:
                        to = (j * chips_x + (i + k) % chips_x) * cores + c
                    else:
                        to = ((j + k) % chips_y * chips_x + i) * cores + c
                    pairs.append(((j * chips_x + i) * cores + c, to))
        return lax.ppermute(part, ROWS_DP, pairs)

    def after(value, *others):
        return lax.optimization_barrier((value,) + others)[0]

    far, far_own = weighted(row_sums, [(1, 2)], [(0, 2)])
    row_sums = after(row_sums, far)
    far = swap(far)
    (near,) = weighted(row_sums, [(1, 1), (1, 3)])
    (far,) = add(add_kernel, "far", [(height, width)], after(far_own, near), far)
    near, row_sums = swap(after(near, far)), after(row_sums, far)
    far = hop(far, 2, 0)
    (near_own,) = weighted(row_sums, [(0, 1), (0, 3)])
    up, down = add(add_kernel, "near", [(height, width)] * 2, near_own, near)
    row_sums = after(row_sums, up)
    up, down = hop(up, 1, 0), hop(down, 3, 0)
    own, part_0 = weighted(row_sums, [(1, 0)], [(0, 0)])
    own = swap(own)
    second_parts = add(
        functools.partial(fold_kernel, chips_y), "fold", [(share, width)] * chips_y, part_0, own, far, up, down
    )
    got = [second_parts[0]] + [hop(second_parts[k], k, 1) for k in (2, 3, 1)]
    tiles = pl.pallas_call(
        finish_kernel,
        in_specs=[VMEM] * len(got),
        out_specs=VMEM,
        out_shape=pltpu.VMEM((owners, SUBLANES, LANES), f32),
        scratch_shapes=[pltpu.VMEM((width, LANES), f32)],
        compiler_params=params(),
        name="finish",
    )(*[resident(part) for part in got])
    tiles = lax.all_to_all(tiles, ROWS_DP, 0, 0)
    placed = pl.pallas_call(
        place_kernel,
        in_specs=[VMEM],
        out_specs=VMEM,
        out_shape=jax.ShapeDtypeStruct((width // owners, local), f32),
        compiler_params=params(),
        name="place",
    )(resident(tiles))
    return placed.T


def solution(mesh):
    clusters = mesh.shape["cluster"]
    sizes = (4, 4, 2, clusters)
    split = Mesh(mesh.devices.reshape(sizes), ROWS_DP + ("cluster",))
    return jax.shard_map(
        functools.partial(per_device, sizes),
        mesh=split,
        in_specs=(P(ROWS_DP, None), P("cluster", None)),
        out_specs=P("cluster", ROWS_DP),
        check_vma=False,
    )
```

```python
import functools

import jax
import jax.numpy as jnp
from jax import lax
from jax.experimental import pallas as pl
from jax.experimental.pallas import tpu as pltpu
from jax.sharding import Mesh
from jax.sharding import PartitionSpec as P

SCALING_PASSES = 3
SOFTNESS_LEVEL = 0.025
LOG2_E = 1.4426950408889634
EXPONENT_SLOPE = LOG2_E / SOFTNESS_LEVEL
ROWS_DP = ("y", "x", "core")
LANES = 128
SUBLANES = 8

VMEM = pl.BlockSpec(memory_space=pltpu.VMEM)


def resident(array):
    return pltpu.with_memory_space_constraint(array, pltpu.VMEM)


def streamed(array):
    return pltpu.with_memory_space_constraint(array, pltpu.HBM)


def params(mebibytes=4):
    return pltpu.CompilerParams(vmem_limit_bytes=mebibytes * 1024 * 1024)


def unit(values):
    values = values.astype(jnp.float32)
    width = values.shape[1]
    factor = lax.rsqrt(jnp.mean(values * values, axis=1, keepdims=True) + 1e-06)
    return (values * factor * width ** (-0.5)).astype(jnp.bfloat16)


def share_order(chips_y, chips_x, share):
    order = []
    for y in range(chips_y):
        for x in range(chips_x):
            order.append((chips_x * y + x) * 2)
    for x in range(chips_x):
        for y in range(chips_y):
            order.append((chips_x * y + x) * 2 + 1)
    return order


def to_lanes(partial_ref, out_ref):
    copies = out_ref.shape[0]
    rows = []
    for group in range(partial_ref.shape[0] // LANES):
        block = partial_ref[group * LANES : (group + 1) * LANES, :]
        rows.append(jnp.sum(block.T, axis=0, keepdims=True))
    total = jnp.concatenate(rows, axis=0)
    for copy in range(copies):
        out_ref[copy] = total


def prepare_kernel(
    order, chunk, embeddings_ref, centroids_ref, kernel_ref, unit_ref, column_ref,
    raw_rows, raw_centroids, unit_centroids, even_rows, odd_rows, even_cosine, odd_cosine, partial, arrived,
):
    share = centroids_ref.shape[0] // len(order)
    chunks = embeddings_ref.shape[0] // chunk

    def fetch(start, size, which):
        rows = pl.ds(start, size)
        return pltpu.make_async_copy(embeddings_ref.at[rows, :], raw_rows.at[rows, :], arrived.at[which])

    pieces = 4
    local = centroids_ref.shape[0]
    height = local // pieces
    fetch_centroids = []
    for piece in range(pieces):
        rows = pl.ds(piece * height, height)
        fetch_centroids.append(
            pltpu.make_async_copy(centroids_ref.at[rows, :], raw_centroids.at[rows, :], arrived.at[piece])
        )
    fetch_first = fetch(0, chunk, pieces)
    fetch_rest = fetch(chunk, embeddings_ref.shape[0] - chunk, pieces + 1)
    for copy in fetch_centroids:
        copy.start()
    fetch_first.start()
    fetch_rest.start()

    def normalise(index, out_ref):
        start = pl.multiple_of(index * chunk, chunk)
        rows = unit(raw_rows[pl.ds(start, chunk), :])
        out_ref[...] = rows
        unit_ref[pl.ds(start, chunk), :] = rows

    def product(rows_ref, out_ref):
        out_ref[...] = lax.dot_general(
            unit_centroids[...], rows_ref[...], (((1,), (1,)), ((), ())), preferred_element_type=jnp.float32
        )

    def exponential(index, cosine_ref):
        start = pl.multiple_of(index * chunk, chunk)
        affinity = jnp.exp2((cosine_ref[...] - 1.0) * EXPONENT_SLOPE)
        kernel_ref[:, pl.ds(start, chunk)] = affinity
        folded = affinity[:, :LANES]
        for tile in range(1, chunk // LANES):
            folded = folded + affinity[:, tile * LANES : (tile + 1) * LANES]
        partial[...] += folded

    for piece in range(pieces):
        fetch_centroids[piece].wait()
        for place, block in enumerate(order):
            if block * share // height == piece:
                unit_centroids[place * share : (place + 1) * share, :] = unit(
                    raw_centroids[block * share : (block + 1) * share, :]
                )
    partial[...] = jnp.zeros_like(partial)
    fetch_first.wait()
    normalise(0, even_rows)
    product(even_rows, even_cosine)
    fetch_rest.wait()
    normalise(1, odd_rows)

    def body(pair, carry):
        index = 2 * pair
        product(odd_rows, odd_cosine)
        exponential(index, even_cosine)
        normalise(index + 2, even_rows)
        product(even_rows, even_cosine)
        exponential(index + 1, odd_cosine)
        normalise(index + 3, odd_rows)
        return carry

    lax.fori_loop(0, chunks // 2 - 1, body, 0)
    product(odd_rows, odd_cosine)
    exponential(chunks - 2, even_cosine)
    exponential(chunks - 1, odd_cosine)
    to_lanes(partial, column_ref)


def row_kernel(target, columns_ref, kernel_ref, row_ref, scale_scratch):
    scale = target / jnp.sum(columns_ref[...], axis=0)
    for group in range(scale.shape[0]):
        scale_scratch[group * LANES : (group + 1) * LANES, :] = jnp.broadcast_to(
            scale[group : group + 1, :], (LANES, LANES)
        ).T
    centroids, rows = kernel_ref.shape
    tiles = rows // LANES
    height = 32

    def body(step, sums):
        start = pl.multiple_of(step * height, height)
        factor = scale_scratch[pl.ds(start, height), :]
        out = []
        for tile in range(tiles):
            product = kernel_ref[pl.ds(start, height), tile * LANES : (tile + 1) * LANES] * factor
            out.append(sums[tile] + jnp.sum(product.reshape(height // SUBLANES, SUBLANES, LANES), axis=0))
        return tuple(out)

    nothing = tuple(jnp.zeros((SUBLANES, LANES), jnp.float32) for _ in range(tiles))
    sums = lax.fori_loop(0, centroids // height, body, nothing, unroll=8)
    total = jnp.concatenate([jnp.sum(tile, axis=0, keepdims=True) for tile in sums], axis=0)
    for copy in range(row_ref.shape[0]):
        row_ref[copy] = total


def column_kernel(rows_ref, kernel_ref, column_ref, partial):
    scale = 1.0 / jnp.sum(rows_ref[...], axis=0)
    centroids, rows = kernel_ref.shape
    tiles = rows // LANES
    height = 32
    factors = [jnp.broadcast_to(scale[tile : tile + 1, :], (SUBLANES, LANES)) for tile in range(tiles)]

    def body(step, carry):
        start = pl.multiple_of(step * height, height)
        total = None
        for tile in range(tiles):
            block = kernel_ref[pl.ds(start, height), tile * LANES : (tile + 1) * LANES]
            product = block.reshape(height // SUBLANES, SUBLANES, LANES) * factors[tile][None]
            total = product if total is None else total + product
        partial[pl.ds(start, height), :] = total.reshape(height, LANES)
        return carry

    lax.fori_loop(0, centroids // height, body, 0, unroll=8)
    to_lanes(partial, column_ref)


def weigh(kernel_ref, scale, weight_scratch, source, place, share):
    tiles = kernel_ref.shape[1] // LANES
    for tile in range(tiles):
        lanes = slice(tile * LANES, (tile + 1) * LANES)
        weight_scratch[place * share : (place + 1) * share, lanes] = (
            kernel_ref[pl.ds(source, share), lanes] * scale[tile : tile + 1, :]
        ).astype(jnp.bfloat16)


def sums_kernel(counts, given, distances, rows_ref, kernel_ref, unit_ref, *rest):
    received, (out_ref, weight_scratch) = rest[:-2], rest[-2:]
    slow, fast = counts
    half = slow * fast
    share = kernel_ref.shape[0] // (2 * half)
    scale = 1.0 / jnp.sum(rows_ref[...], axis=0)
    y, x, core = (lax.axis_index(name) for name in ROWS_DP)
    base = 1 - core if given else core
    first, second = jnp.where(base == 0, y, x), jnp.where(base == 0, x, y)
    for part, a in enumerate(distances):
        for b in range(fast):
            block = base * half + lax.rem(first + a, slow) * fast + lax.rem(second + b, fast)
            weigh(kernel_ref, scale, weight_scratch, pl.multiple_of(block * share, share), part * fast + b, share)
    height = 128
    for part in range(weight_scratch.shape[0] // height):
        rows = slice(part * height, (part + 1) * height)
        sums = jnp.dot(weight_scratch[rows, :], unit_ref[...], preferred_element_type=jnp.float32)
        out_ref[rows, :] = sums + received[0][rows, :] if received else sums


def add_kernel(own_ref, other_ref, *outs):
    height = outs[0].shape[0]
    for part, out_ref in enumerate(outs):
        rows = slice(part * height, (part + 1) * height)
        out_ref[...] = own_ref[rows, :] + other_ref[rows, :]


def fold_kernel(parts, *refs):
    ins, outs = refs[:-parts], refs[-parts:]
    share = outs[0].shape[0]
    for part in range(parts):
        rows = slice(part * share, (part + 1) * share)
        total = ins[0][rows, :]
        for other in ins[1:]:
            total = total + other[rows, :]
        outs[part][...] = total


def finish_kernel(*refs):
    ins, out_ref, turned = refs[:-2], refs[-2], refs[-1]
    total = ins[0][...]
    for other in ins[1:]:
        total = total + other[...]
    share, width = total.shape
    factor = lax.rsqrt(jnp.mean(total * total, axis=1, keepdims=True) + 1e-06)
    total = total * factor
    repeated = jnp.concatenate([total] * (LANES // share), axis=0)
    for group in range(width // LANES):
        turned[group * LANES : (group + 1) * LANES, :] = repeated[:, group * LANES : (group + 1) * LANES].T
    slab = lax.broadcasted_iota(jnp.int32, (SUBLANES, LANES), 1) // share
    features = width // out_ref.shape[0]
    slabs = features // SUBLANES
    for owner in range(out_ref.shape[0]):
        tile = turned[owner * features : owner * features + SUBLANES, :]
        for j in range(1, slabs):
            start = owner * features + j * SUBLANES
            tile = jnp.where(slab == j, turned[start : start + SUBLANES, :], tile)
        out_ref[owner] = tile


def place_kernel(tiles_ref, out_ref):
    owners = tiles_ref.shape[0]
    features, centroids = out_ref.shape
    share = centroids // owners
    per = LANES // share
    slab = lax.broadcasted_iota(jnp.int32, (SUBLANES, LANES), 1) // share
    for group in range(owners // per):
        for j in range(features // SUBLANES):
            made = None
            for s in range(per):
                tile = tiles_ref[group * per + s]
                shift = (share * (s - j)) % LANES
                moved = pltpu.roll(tile, shift, 1) if shift else tile
                made = moved if made is None else jnp.where(slab == s, moved, made)
            out_ref[j * SUBLANES : (j + 1) * SUBLANES, group * LANES : (group + 1) * LANES] = made


def ring(count, step):
    return [(i, (i + step) % count) for i in range(count)]


def per_device(sizes, embeddings, centroids):
    chips_y, chips_x, cores, clusters = sizes
    owners = chips_y * chips_x * cores
    rows, width = embeddings.shape
    local = centroids.shape[0]
    share = local // owners
    target = rows * owners / (local * clusters)
    order = share_order(chips_y, chips_x, share)
    f32, bf16 = jnp.float32, jnp.bfloat16
    chunk = 512

    kernel, unit_rows, columns = pl.pallas_call(
        functools.partial(prepare_kernel, order, chunk),
        in_specs=[pl.BlockSpec(memory_space=pltpu.HBM)] * 2,
        out_specs=[VMEM, VMEM, VMEM],
        out_shape=[
            pltpu.VMEM((local, rows), f32),
            pltpu.VMEM((rows, width), bf16),
            pltpu.VMEM((owners, local // LANES, LANES), f32),
        ],
        scratch_shapes=[
            pltpu.VMEM((rows, width), bf16),
            pltpu.VMEM((local, width), bf16),
            pltpu.VMEM((local, width), bf16),
            pltpu.VMEM((chunk, width), bf16),
            pltpu.VMEM((chunk, width), bf16),
            pltpu.VMEM((local, chunk), f32),
            pltpu.VMEM((local, chunk), f32),
            pltpu.VMEM((local, LANES), f32),
            pltpu.SemaphoreType.DMA((6,)),
        ],
        compiler_params=params(24),
        name="prepare",
    )(streamed(embeddings), streamed(centroids))

    def column_exchange(sums):
        return lax.all_to_all(sums, ROWS_DP, 0, 0)

    def row_exchange(sums):
        return lax.all_to_all(sums, "cluster", 0, 0)

    for sweep in range(SCALING_PASSES):
        if sweep:
            columns = pl.pallas_call(
                column_kernel,
                in_specs=[VMEM, VMEM],
                out_specs=VMEM,
                out_shape=pltpu.VMEM((owners, local // LANES, LANES), f32),
                scratch_shapes=[pltpu.VMEM((local, LANES), f32)],
                compiler_params=params(),
                name="columns",
            )(resident(row_sums), resident(kernel))
        columns = column_exchange(columns)
        row_sums = pl.pallas_call(
            functools.partial(row_kernel, target),
            in_specs=[VMEM, VMEM],
            out_specs=VMEM,
            out_shape=pltpu.VMEM((clusters, rows // LANES, LANES), f32),
            scratch_shapes=[pltpu.VMEM((local, LANES), f32)],
            compiler_params=params(),
            name="rows",
        )(resident(columns), resident(kernel))
        row_sums = row_exchange(row_sums)

    height = chips_y * share

    def weighted(row_sums, given, distances, *received):
        count = len(distances)
        return pl.pallas_call(
            functools.partial(sums_kernel, (chips_x, chips_y), given, distances),
            in_specs=[VMEM] * (3 + len(received)),
            out_specs=VMEM,
            out_shape=pltpu.VMEM((count * height, width), f32),
            scratch_shapes=[pltpu.VMEM((count * height, rows), bf16)],
            compiler_params=params(6),
            cost_estimate=pl.CostEstimate(
                flops=2 * count * height * rows * width,
                bytes_accessed=4 * count * height * (rows + width),
                transcendentals=0,
            ),
            name="sums",
        )(resident(row_sums), resident(kernel), resident(unit_rows), *[resident(part) for part in received])

    def add(body, name, shapes, *arrays):
        return pl.pallas_call(
            body,
            in_specs=[VMEM] * len(arrays),
            out_specs=[VMEM] * len(shapes),
            out_shape=[pltpu.VMEM(shape, f32) for shape in shapes],
            compiler_params=params(),
            name=name,
        )(*[resident(array) for array in arrays])

    def swap(part):
        return lax.ppermute(part, "core", ring(2, 1))

    def hop(part, k, x_core):
        pairs = []
        for j in range(chips_y):
            for i in range(chips_x):
                for c in range(cores):
                    if c == x_core:
                        to = (j * chips_x + (i + k) % chips_x) * cores + c
                    else:
                        to = ((j + k) % chips_y * chips_x + i) * cores + c
                    pairs.append(((j * chips_x + i) * cores + c, to))
        return lax.ppermute(part, ROWS_DP, pairs)

    def after(value, *others):
        return lax.optimization_barrier((value,) + others)[0]

    far = weighted(row_sums, True, (2,))
    row_sums = after(row_sums, far)
    far = swap(far)
    near = weighted(row_sums, True, (1, 3))
    row_sums = after(row_sums, near)
    far = weighted(row_sums, False, (2,), far)
    near = swap(after(near, far))
    row_sums = after(row_sums, far)
    far = hop(far, 2, 1)
    near_own = weighted(row_sums, False, (1, 3))
    up, down = add(add_kernel, "near", [(height, width)] * 2, near_own, near)
    row_sums = after(row_sums, up)
    up, down = hop(up, 1, 1), hop(down, 3, 1)
    own = weighted(row_sums, True, (0,))
    row_sums = after(row_sums, own)
    own = swap(own)
    part_0 = weighted(row_sums, False, (0,))
    second_parts = add(
        functools.partial(fold_kernel, chips_y), "fold", [(share, width)] * chips_y, part_0, own, far, up, down
    )
    got = [second_parts[0]] + [hop(second_parts[k], k, 0) for k in (2, 3, 1)]
    tiles = pl.pallas_call(
        finish_kernel,
        in_specs=[VMEM] * len(got),
        out_specs=VMEM,
        out_shape=pltpu.VMEM((owners, SUBLANES, LANES), f32),
        scratch_shapes=[pltpu.VMEM((width, LANES), f32)],
        compiler_params=params(),
        name="finish",
    )(*[resident(part) for part in got])
    tiles = lax.all_to_all(tiles, ROWS_DP, 0, 0)
    placed = pl.pallas_call(
        place_kernel,
        in_specs=[VMEM],
        out_specs=VMEM,
        out_shape=jax.ShapeDtypeStruct((width // owners, local), f32),
        compiler_params=params(),
        name="place",
    )(resident(tiles))
    return placed.T


def solution(mesh):
    clusters = mesh.shape["cluster"]
    sizes = (4, 4, 2, clusters)
    split = Mesh(mesh.devices.reshape(sizes), ROWS_DP + ("cluster",))
    return jax.shard_map(
        functools.partial(per_device, sizes),
        mesh=split,
        in_specs=(P(ROWS_DP, None), P("cluster", None)),
        out_specs=P("cluster", ROWS_DP),
        check_vma=False,
    )
```
